32 devices in a mesh: member: 2 (over x), lat: 16 (over z, y, core).
Axes of the slice: x: 2, y: 2, z: 4, core: 2. Of those that a mesh axis runs over, the one named last changes fastest.
Arguments:
- state: float32 [256, 32, 1152], P('member', 'lat'), parts along dimension 0, may hold values from -6 to 6
- vertical_mix: float32 [8, 16, 16], replicated, may hold values from -1.5 to 1.5
- coupling: float32 [4, 8], replicated, may hold values from -2 to 2
- fractions: float32 [16, 1152], replicated, may hold values from 0.25 to 1
- weight_index: int32 [64], P(('member', 'lat')), parts along dimension 0, may hold values from 0 to 15
- band_bounds: int32 [17], replicated, may hold values from 0 to 32, as said below
- polar_mask: int32 [32], replicated, may hold values from 0 to 1, as said below
Outputs:
- state_out: float32 [256, 32, 1152], P(('member', 'lat')), parts along dimension 0
- ocean: float32 [4, 192, 1152], P(None, ('member', 'lat')), parts along dimension 1
The draws below stay inside these ranges and needn't reach their ends.
There are 2 independent parts, one for each index of `member`. The reference program is written for one: setup_inputs(seed, part) draws one part's arguments, and reference() takes and returns one part's arrays. A program takes and returns all parts, laid end to end along the dimension named above; an argument that names none is the same for every part. Nothing has to cross between parts.
Inputs may be any that keep to these rules, and one draw needn't show every extreme that they name: `band_bounds`: starts at 0, ends at 32; entry o lies between o * 2 - 2/2 and o * 2 + 2/2 - 1; some owner's slots hold exactly 6 rows. `polar_mask`: 0 outside the first and the last 5 rows; 1 on rows 4 and 27.
All inputs are finite; a program needn't handle non-finite values.
Results may differ from the reference program's by a relative error of at most 0.00007.
Values sent between devices are 32-bit elements; how exact they have to be, the bound alone decides.
No kernel may reach another device: no remote copies, remote signals or barrier semaphores. Data moves between devices by JAX's collectives and lax.ppermute only.
A program may use at most 64 MiB of HBM per device.

```python
import jax
import jax.numpy as jnp
from jax import lax

F = 8
LEV = 16
NLON = 1152
ROWS_DEV = 2
NFLUX = 4
NW = 16
NLAT = 32
FL = 128
POLAR = 5
N_LAT = 16


def draw_band_bounds(key, part):
    key = jax.random.fold_in(key, 11)
    half_rows = ROWS_DEV // 2
    first_key, second_key = jax.random.split(key)
    offsets = jax.random.randint(first_key, (N_LAT + 1,), -half_rows, half_rows)
    where_wide = jax.random.randint(second_key, (), 1, N_LAT - 1)
    offsets = offsets.at[where_wide].set(-half_rows)
    offsets = offsets.at[where_wide + 1].set(half_rows - 1)
    offsets = offsets.at[0].set(0)
    offsets = offsets.at[N_LAT].set(0)
    return (ROWS_DEV * jnp.arange(N_LAT + 1, dtype=jnp.int32) + offsets).astype(jnp.int32)


def draw_polar_mask(key, part):
    key = jax.random.fold_in(key, 23)
    row_index = jnp.arange(NLAT, dtype=jnp.int32)
    in_caps = (row_index < POLAR) | (row_index >= NLAT - POLAR)
    cap_edge = (row_index == POLAR - 1) | (row_index == NLAT - POLAR)
    chosen = jax.random.randint(key, (NLAT,), 0, 4) > 0
    return jnp.where(cap_edge | in_caps & chosen, 1, 0).astype(jnp.int32)


def plant(drawn, stream_key, smallest, high):
    index_at = [jax.random.randint(jax.random.fold_in(stream_key, axis), (), 0, length) for axis, length in enumerate(drawn.shape)]
    widest = drawn.shape.index(max(drawn.shape))
    neighbour = index_at[:widest] + [(index_at[widest] + 1) % drawn.shape[widest]] + index_at[widest + 1:]
    return drawn.at[tuple(index_at)].set(smallest).at[tuple(neighbour)].set(high)


def levels(key, shape, cuts, smallest, largest):
    def one(dim, shards_of):
        steps = jax.random.uniform(jax.random.fold_in(jax.random.fold_in(key, 6), dim), (shards_of,), jnp.float32, smallest / len(cuts), largest / len(cuts))
        return jnp.repeat(jnp.exp(steps), shape[dim] // shards_of).reshape((-1,) + (1,) * (len(shape) - dim - 1))

    level = one(*cuts[0])
    for cut in cuts[1:]:
        level = level * one(*cut)
    return level


def scatter_about(key, dims, scale, limit, shards=(), kind=jnp.bfloat16):
    entries = scale * jax.random.normal(key, dims, jnp.float32)
    if shards:
        entries = entries * levels(key, dims, shards, -0.22, 0.18)
    return jnp.clip(entries, -limit, limit).astype(kind)


def setup_inputs(seed: int = 0, part: int = 0) -> dict:
    seeds = jax.random.split(jax.random.key(seed), 8)
    part_splits = jax.random.split(jax.random.fold_in(seeds[7], part), 8)
    return {
        "state": scatter_about(part_splits[0], (FL, NLAT, NLON), 1.0, 6.0, ((1, 16),), jnp.float32),
        "vertical_mix": scatter_about(seeds[1], (F, LEV, LEV), LEV ** -0.5, 1.5, (), jnp.float32),
        "coupling": scatter_about(seeds[2], (NFLUX, F), F ** -0.5, 2.0, (), jnp.float32),
        "fractions": jnp.clip(jax.random.uniform(seeds[3], (NW, NLON), jnp.float32, 0.25, 1.0), 0.25, 1.0),
        "weight_index": plant(jax.random.randint(part_splits[4], (NLAT,), 0, NW), jax.random.fold_in(part_splits[4], 1), 0, NW - 1).astype(jnp.int32),
        "band_bounds": draw_band_bounds(jax.random.fold_in(seeds[7], 71), part),
        "polar_mask": draw_polar_mask(jax.random.fold_in(seeds[7], 71), part),
    }


COSCUT = 0.5
HIGHEST = lax.Precision.HIGHEST

def damping_table(lat_count, lon_count):
    latitude = jnp.pi * ((jnp.arange(lat_count).astype(jnp.float32) + 0.5) / lat_count - 0.5)
    cos_square = jnp.cos(latitude) ** 2
    wavenumber = jnp.arange(lon_count // 2 + 1).astype(jnp.float32)
    sin_square = jnp.sin(jnp.pi * wavenumber / lon_count) ** 2
    return cos_square[:, None] / jnp.maximum(cos_square[:, None], COSCUT ** 2 * sin_square[None, :])

def reference(state, vertical_mix, coupling, fractions, weight_index, band_bounds, polar_mask):
    columns = state.reshape(F, LEV, NLAT * NLON)
    mixed_state = jnp.einsum('fkl,flc->fkc', vertical_mix, columns, precision=HIGHEST)
    bottom = mixed_state[:, LEV - 1]
    wind_speed = jnp.sqrt(bottom[0] ** 2 + bottom[1] ** 2 + 1.0)
    surface_flux = wind_speed[None, :] * jnp.dot(coupling, bottom, precision=HIGHEST)
    onehot = (weight_index[:, None] == jnp.arange(NW, dtype=jnp.int32)[None, :]).astype(jnp.float32)
    row_fraction = jnp.dot(onehot, fractions, precision=HIGHEST)
    weighted = surface_flux.reshape(NFLUX, NLAT, NLON) * row_fraction[None]
    half_rows = ROWS_DEV // 2
    slot_index = jnp.arange(3 * ROWS_DEV, dtype=jnp.int32)
    band_start = band_bounds[:-1] - half_rows
    band_length = band_bounds[1:] - band_bounds[:-1] + 2 * half_rows + 1
    raw_rows = (band_start[:, None] + slot_index[None, :]).astype(jnp.int32)
    source_rows = jnp.clip(raw_rows, 0, NLAT - 1).astype(jnp.int32)
    valid_slot = (slot_index[None, :] < band_length[:, None]) & (raw_rows >= 0) & (raw_rows < NLAT)
    picked = jnp.take(weighted, source_rows.reshape(-1), axis=1).reshape(NFLUX, N_LAT, 3 * ROWS_DEV, NLON)
    ocean = jnp.where(valid_slot[None, :, :, None], picked, 0.0).reshape(NFLUX, N_LAT * 3 * ROWS_DEV, NLON)
    damping = jnp.where(polar_mask[:, None] == 1, damping_table(NLAT, NLON), 1.0)
    stacked = mixed_state.reshape(FL, NLAT, NLON)

    def filter_one(values):
        spectrum = jnp.fft.rfft(values, axis=-1) * damping
        return jnp.fft.irfft(spectrum, n=NLON, axis=-1)
    state_out = lax.map(filter_one, stacked)
    return (state_out, ocean)
```

```python
import functools

import jax
import jax.numpy as jnp
import numpy as np
from jax import lax
from jax.experimental import pallas as pl
from jax.experimental.pallas import tpu as pltpu
from jax.sharding import PartitionSpec as P

COSCUT = 0.5
LANES = 128
ORDER = (12, 8, 4, 2, 13, 9, 5, 1, 14, 10, 6, 3, 15, 11, 7)
F32 = jnp.float32
BF16 = jnp.bfloat16


def split_product(left, right, dims=(((1,), (0,)), ((), ()))):
    high = left.astype(BF16)
    low = (left - high.astype(F32)).astype(BF16)
    dot = functools.partial(lax.dot_general, dimension_numbers=dims, preferred_element_type=F32)
    return dot(high, right[0]) + (dot(high, right[1]) + dot(low, right[0]))


def halves(values):
    high = values.astype(BF16)
    return high, (values - high.astype(F32)).astype(BF16)


def np_halves(values):
    values = np.asarray(values, np.float32)
    high = values.astype(jnp.bfloat16)
    return np.stack([high, (values - high.astype(np.float32)).astype(jnp.bfloat16)])


def transform_tables(lon_count):
    radix = lon_count // LANES
    b = np.arange(LANES)[:, None]
    k2 = np.arange(LANES)[None, :]
    steps = []
    for k in range(1, radix // 2 + 1):
        angle = 2 * np.pi * ((b * (k + radix * k2)) % lon_count) / lon_count
        c, s = np.cos(angle), np.sin(angle)
        steps.append(np.block([[c, -s], [s, c]]))
    half = LANES // 2
    angle0 = 2 * np.pi * ((b * k2) % LANES) / LANES
    first = np.concatenate(
        [np.cos(angle0[:, : half + 1]), np.sin(angle0[:, 1:half])], axis=1
    )
    wave0 = np.concatenate([np.arange(half + 1), np.arange(1, half)]) * radix
    scale0 = np.where(wave0 * 2 % lon_count == 0, 1.0, 2.0) / lon_count
    waves = [np.concatenate([wave0, np.zeros(LANES)])]
    scales = [np.concatenate([scale0, np.zeros(LANES)])]
    for k in range(1, radix // 2 + 1):
        one = k + radix * np.arange(LANES)
        waves.append(np.concatenate([one, one]))
        scales.append(np.full(2 * LANES, 2.0 / lon_count))
    limit = COSCUT**2 * np.sin(np.pi * np.stack(waves) / lon_count) ** 2
    return (
        np_halves(np.stack(steps)),
        np_halves(first),
        limit.astype(np.float32),
        np.stack(scales).astype(np.float32),
    )


def row_cos_square(lat_count):
    latitude = np.pi * ((np.arange(lat_count) + 0.5) / lat_count - 0.5)
    return (np.cos(latitude) ** 2).astype(np.float32)


def filtered(fields, cos_square, step_table, first_table, limit, scale):
    radix = fields.shape[1] // LANES
    half = radix // 2
    parts = [fields[:, a * LANES : (a + 1) * LANES] for a in range(radix)]
    sums = [parts[a] + parts[radix - a] for a in range(1, half + 1)]
    gaps = [parts[a] - parts[radix - a] for a in range(1, half + 1)]
    back = (((1,), (1,)), ((), ()))

    def gain(k, width):
        return (
            cos_square / jnp.maximum(cos_square, limit[k : k + 1, :width]) * scale[k : k + 1, :width]
        )

    total = parts[0]
    for value in sums:
        total = total + value
    pair = (first_table[0], first_table[1])
    spectrum = split_product(total, pair) * gain(0, LANES)
    base = split_product(spectrum, pair, back)
    cosines, sines = [], []
    for k in range(1, half + 1):
        real, imag = parts[0], None
        for a in range(1, half + 1):
            angle = 2 * np.pi * (a * k % radix) / radix
            real = real + float(np.cos(angle)) * sums[a - 1]
            term = float(-np.sin(angle)) * gaps[a - 1]
            imag = term if imag is None else imag + term
        pair = (step_table[0, k - 1], step_table[1, k - 1])
        spectrum = split_product(jnp.concatenate([real, imag], axis=1), pair) * gain(k, 2 * LANES)
        series = split_product(spectrum, pair, back)
        cosines.append(series[:, :LANES])
        sines.append(series[:, LANES:])
    whole = base
    for value in cosines:
        whole = whole + value
    out = [whole]
    lower, upper = [], []
    for a in range(1, half + 1):
        even, odd = base, None
        for k in range(1, half + 1):
            angle = 2 * np.pi * (a * k % radix) / radix
            even = even + float(np.cos(angle)) * cosines[k - 1]
            term = float(np.sin(angle)) * sines[k - 1]
            odd = term if odd is None else odd + term
        lower.append(even - odd)
        upper.append(even + odd)
    return jnp.concatenate(out + lower + upper[::-1], axis=1)


def mix_kernel(masks, swap, state_ref, mix_ref, mask_ref, cos_ref, steps_ref, first_ref, limit_ref, scale_ref, *refs):
    out_refs, (load_ref, sem) = refs[:-2], refs[-2:]
    levels = mix_ref.shape[1]
    rows, lon = state_ref.shape[1:]
    part = out_refs[0].shape[1]
    split = levels // part
    me = lax.axis_index("lat")
    chip = me // split
    core = lax.rem(me, split)
    fields = [jnp.bitwise_xor(chip, mask) if swap else mask for mask in masks]
    copies = [
        pltpu.make_async_copy(
            state_ref.at[pl.ds(field * levels, levels)], load_ref.at[i], sem.at[i]
        )
        for i, field in enumerate(fields)
    ]
    for copy in copies:
        copy.start()
    for i, field in enumerate(fields):
        weights = jnp.concatenate(
            [
                mix_ref[field, pl.ds(pl.multiple_of((jnp.bitwise_xor(core, c) if swap else c) * part, part), part), :]
                for c in range(split)
            ],
            axis=0,
        )
        copies[i].wait()
        for r in range(rows):
            mixed = split_product(weights, halves(load_ref[i, :, r, :]))
            for c in range(split):
                out_refs[i * split + c][r] = mixed[c * part : (c + 1) * part]
    active = [mask_ref[me * rows + r] == 1 for r in range(rows)]

    @pl.when(functools.reduce(jnp.logical_or, active))
    def _():
        height = len(out_refs) * part
        fields = jnp.concatenate([ref[r] for r in range(rows) for ref in out_refs], axis=0)
        cos_square = jnp.concatenate(
            [jnp.full((height, 1), cos_ref[me * rows + r], F32) for r in range(rows)], axis=0
        )
        smooth = filtered(fields, cos_square, steps_ref, first_ref, limit_ref, scale_ref)
        for r in range(rows):

            @pl.when(active[r])
            def _():
                for i, ref in enumerate(out_refs):
                    start = r * height + i * part
                    ref[r] = smooth[start : start + part]


def mix(state, vertical_mix, polar_mask, tables, masks, part, swap):
    stack_count, rows, lon = state.shape
    levels = vertical_mix.shape[1]
    outs = len(masks) * (levels // part)
    vmem = pl.BlockSpec(memory_space=pltpu.VMEM)
    smem = pl.BlockSpec(memory_space=pltpu.SMEM)
    return pl.pallas_call(
        functools.partial(mix_kernel, masks, swap),
        out_shape=[jax.ShapeDtypeStruct((rows, part, lon), F32)] * outs,
        in_specs=[pl.BlockSpec(memory_space=pl.ANY), vmem, smem, smem, vmem, vmem, vmem, vmem],
        out_specs=[vmem] * outs,
        scratch_shapes=[
            pltpu.VMEM((len(masks), levels, rows, lon), F32),
            pltpu.SemaphoreType.DMA((len(masks),)),
        ],
        compiler_params=pltpu.CompilerParams(vmem_limit_bytes=40 << 20),
        name="mix",
    )(state, vertical_mix, polar_mask, *tables)


def flux_kernel(state_ref, mix_ref, coupling_ref, fractions_ref, index_ref, out_ref):
    fields, levels, _ = mix_ref.shape
    rows = state_ref.shape[1]
    for r in range(rows):
        bottom = jnp.concatenate(
            [
                split_product(
                    mix_ref[f, levels - 8 : levels, :],
                    halves(state_ref[f * levels : (f + 1) * levels, r, :]),
                )[7:8]
                for f in range(fields)
            ],
            axis=0,
        )
        speed = jnp.sqrt(bottom[0:1] * bottom[0:1] + bottom[1:2] * bottom[1:2] + 1.0)
        flux = jnp.dot(
            coupling_ref[...], bottom, precision=lax.Precision.HIGHEST, preferred_element_type=F32
        )
        out_ref[r] = speed * flux * fractions_ref[pl.ds(index_ref[r], 1), :]


def surface_flux(state, vertical_mix, coupling, fractions, weight_index):
    vmem = pl.BlockSpec(memory_space=pltpu.VMEM)
    return pl.pallas_call(
        flux_kernel,
        out_shape=jax.ShapeDtypeStruct((state.shape[1], coupling.shape[0], state.shape[2]), F32),
        in_specs=[vmem] * 4 + [pl.BlockSpec(memory_space=pltpu.SMEM)],
        out_specs=vmem,
        compiler_params=pltpu.CompilerParams(vmem_limit_bytes=40 << 20),
        name="flux",
    )(state, vertical_mix, coupling, fractions, weight_index)


def ocean_kernel(lat_count, bounds_ref, left_ref, own_ref, right_ref, out_ref):
    rows = own_ref.shape[0]
    slots = out_ref.shape[0]
    half = rows // 2
    me = lax.axis_index("lat")
    start = bounds_ref[me] - half
    length = bounds_ref[me + 1] - bounds_ref[me] + 2 * half + 1
    shift = start - (me - 1) * rows
    near = [ref[r] for ref in (left_ref, own_ref, right_ref) for r in range(rows)]
    for s in range(slots):
        row = start + s
        valid = (s < length) & (row >= 0) & (row < lat_count)
        picked = jnp.zeros_like(near[0])
        for p, value in enumerate(near):
            picked = jnp.where(valid & (shift + s == p), value, picked)
        out_ref[s] = picked


def ocean_slots(weighted, band_bounds, lat_count, device_count):
    rows, flux_count, lon = weighted.shape
    ends = device_count - 1
    left = lax.ppermute(weighted, "lat", [(i, i + 1) for i in range(ends)])
    right = lax.ppermute(weighted, "lat", [(i + 1, i) for i in range(ends)])
    vmem = pl.BlockSpec(memory_space=pltpu.VMEM)
    slots = pl.pallas_call(
        functools.partial(ocean_kernel, lat_count),
        out_shape=jax.ShapeDtypeStruct((3 * rows, flux_count, lon), F32),
        in_specs=[pl.BlockSpec(memory_space=pltpu.SMEM)] + [vmem] * 3,
        out_specs=vmem,
        name="ocean",
    )(band_bounds, left, weighted, right)
    return jnp.transpose(slots, (1, 0, 2))


def place_kernel(*refs):
    in_refs, out_ref = refs[:-1], refs[-1]
    rows = in_refs[0].shape[0]
    me = lax.axis_index("lat")
    for m, ref in enumerate(in_refs):
        start = jnp.bitwise_xor(me, m) * rows
        for r in range(rows):
            out_ref[:, pl.ds(start + r, 1), :] = ref[r][:, None, :]


def place(blocks, lat_count):
    rows, part, lon = blocks[0].shape
    vmem = pl.BlockSpec(memory_space=pltpu.VMEM)
    return pl.pallas_call(
        place_kernel,
        out_shape=jax.ShapeDtypeStruct((part, lat_count, lon), F32),
        in_specs=[vmem] * len(blocks),
        out_specs=vmem,
        compiler_params=pltpu.CompilerParams(vmem_limit_bytes=40 << 20),
        name="place",
    )(*blocks)


def body(device_count, state, vertical_mix, coupling, fractions, weight_index, band_bounds, polar_mask):
    field_count, level_count = vertical_mix.shape[:2]
    stack_count, row_count, lon_count = state.shape
    lat_count = polar_mask.shape[0]
    part = stack_count // device_count
    steps, first, limit, scale = transform_tables(lon_count)
    tables = (row_cos_square(lat_count), steps, first, limit, scale)
    weighted = surface_flux(state, vertical_mix, coupling, fractions, weight_index)
    if part % 8 == 0 and device_count == len(ORDER) + 1:
        split = level_count // part
        blocks = mix(state, vertical_mix, polar_mask, tables, tuple(range(field_count)), part, True)
        received = {0: blocks[0]}
        for m in reversed(ORDER):
            received[m] = lax.ppermute(
                blocks[m], "lat", [(i, i ^ m) for i in range(device_count)]
            )
        state_out = place([received[m] for m in range(device_count)], lat_count)
    else:
        mixed = mix(
            state, vertical_mix, polar_mask, tables, tuple(range(field_count)), level_count, False
        )
        stacked = jnp.concatenate(mixed, axis=1)
        moved = lax.all_to_all(stacked, "lat", split_axis=1, concat_axis=0, tiled=True)
        state_out = jnp.transpose(moved, (1, 0, 2))
    ocean = ocean_slots(weighted, band_bounds, lat_count, device_count)
    return (state_out, ocean)


def solution(mesh):
    return jax.shard_map(
        functools.partial(body, mesh.shape["lat"]),
        mesh=mesh,
        in_specs=(P("member", "lat", None), P(), P(), P(), P(("member", "lat")), P(), P()),
        out_specs=(P(("member", "lat"), None, None), P(None, ("member", "lat"), None)),
        check_vma=False,
    )
```

```python
import functools

import jax
import jax.numpy as jnp
import numpy as np
from jax import lax
from jax.experimental import pallas as pl
from jax.experimental.pallas import tpu as pltpu
from jax.sharding import PartitionSpec as P

COSCUT = 0.5
LANES = 128
SUBLANES = 8
DIRECT = 6
BUNDLES = (5, 7, 3, 4, 1, 2)
F32 = jnp.float32
BF16 = jnp.bfloat16
NORMAL = (((1,), (0,)), ((), ()))
TRANSPOSED = (((1,), (1,)), ((), ()))
VMEM_LIMIT = 48 << 20


def halves(values):
    high = values.astype(BF16)
    return high, (values - high.astype(F32)).astype(BF16)


def split_product(left, right, dims=NORMAL):
    dot = functools.partial(lax.dot_general, dimension_numbers=dims, preferred_element_type=F32)
    return dot(left[0], right[0]) + (dot(left[0], right[1]) + dot(left[1], right[0]))


def np_halves(values):
    values = np.asarray(values, np.float32)
    high = values.astype(jnp.bfloat16)
    return np.stack([high, (values - high.astype(np.float32)).astype(jnp.bfloat16)])


def transform_tables(lon_count, lat_count):
    radix = lon_count // LANES
    steps = radix // 2
    b = np.arange(LANES)[:, None]
    k2 = np.arange(LANES)[None, :]
    table = np.zeros((steps * 2 * LANES + LANES, 2 * LANES))
    for k in range(1, steps + 1):
        angle = 2 * np.pi * ((b * (k + radix * k2)) % lon_count) / lon_count
        c, s = np.cos(angle), np.sin(angle)
        table[(k - 1) * 2 * LANES : k * 2 * LANES] = np.block([[c, -s], [s, c]])
    half = LANES // 2
    angle = 2 * np.pi * ((b * k2) % LANES) / LANES
    table[steps * 2 * LANES :, :LANES] = np.concatenate(
        [np.cos(angle[:, : half + 1]), np.sin(angle[:, 1:half])], axis=1
    )
    wave = np.zeros((steps + 1, 2 * LANES))
    scale = np.full((steps + 1, 2 * LANES), 2.0 / lon_count)
    wave[0, :LANES] = np.concatenate([np.arange(half + 1), np.arange(1, half)]) * radix
    scale[0, [0, half]] = 1.0 / lon_count
    for k in range(1, steps + 1):
        wave[k] = np.tile(k + radix * np.arange(LANES), 2)
    limit = COSCUT**2 * np.sin(np.pi * wave / lon_count) ** 2
    latitude = np.pi * ((np.arange(lat_count) + 0.5) / lat_count - 0.5)
    square = np.repeat(np.cos(latitude)[:, None] ** 2, 2 * LANES, axis=1)
    rows = np.concatenate([limit, scale, square])
    rows = np.pad(rows, ((0, -len(rows) % SUBLANES), (0, 0)))
    return np_halves(table), rows.astype(np.float32)


def filtered(fields, squares, table_ref, row_ref):
    radix = fields.shape[1] // LANES
    half = radix // 2
    height = fields.shape[0] // len(squares)
    parts = [fields[:, a * LANES : (a + 1) * LANES] for a in range(radix)]
    sums = [parts[a] + parts[radix - a] for a in range(1, half + 1)]
    gaps = [parts[a] - parts[radix - a] for a in range(1, half + 1)]

    def pair(k):
        if k == 0:
            rows, width = slice(half * 2 * LANES, half * 2 * LANES + LANES), LANES
        else:
            rows, width = slice((k - 1) * 2 * LANES, k * 2 * LANES), 2 * LANES
        return table_ref[0, rows, :width], table_ref[1, rows, :width]

    def gain(k, width):
        limit = row_ref[k : k + 1, :LANES]
        scale = row_ref[half + 1 + k : half + 2 + k, :LANES]
        groups = [
            jnp.broadcast_to(square / jnp.maximum(square, limit) * scale, (height, LANES))
            for square in squares
        ]
        groups = jnp.concatenate(groups, axis=0)
        return groups if width == LANES else jnp.concatenate([groups, groups], axis=1)

    total = parts[0]
    for value in sums:
        total = total + value
    spectrum = split_product(halves(total), pair(0)) * gain(0, LANES)
    base = split_product(halves(spectrum), pair(0), TRANSPOSED)
    cosines, sines = [], []
    for k in range(1, half + 1):
        real, imag = parts[0], None
        for a in range(1, half + 1):
            angle = 2 * np.pi * (a * k % radix) / radix
            real = real + float(np.cos(angle)) * sums[a - 1]
            term = float(-np.sin(angle)) * gaps[a - 1]
            imag = term if imag is None else imag + term
        both = jnp.concatenate([real, imag], axis=1)
        spectrum = split_product(halves(both), pair(k)) * gain(k, 2 * LANES)
        series = split_product(halves(spectrum), pair(k), TRANSPOSED)
        cosines.append(series[:, :LANES])
        sines.append(series[:, LANES:])
    whole = base
    for value in cosines:
        whole = whole + value
    lower, upper = [], []
    for a in range(1, half + 1):
        even, odd = base, None
        for k in range(1, half + 1):
            angle = 2 * np.pi * (a * k % radix) / radix
            even = even + float(np.cos(angle)) * cosines[k - 1]
            term = float(np.sin(angle)) * sines[k - 1]
            odd = term if odd is None else odd + term
        lower.append(even - odd)
        upper.append(even + odd)
    return jnp.concatenate([whole] + lower + upper[::-1], axis=1)


def filter_blocks(rows, out_refs, mask_ref, table_ref, row_ref, table_copy):
    part = out_refs[0].shape[1]
    height = len(out_refs) * part
    radix = out_refs[0].shape[2] // LANES
    first_square = 2 * (radix // 2 + 1)
    active = [mask_ref[row] == 1 for row in rows]
    table_copy.wait()

    @pl.when(functools.reduce(jnp.logical_or, active))
    def _():
        fields = jnp.concatenate([ref[r] for r in range(len(rows)) for ref in out_refs], axis=0)
        squares = [row_ref[pl.ds(first_square + row, 1), :][:, :LANES] for row in rows]
        smooth = filtered(fields, squares, table_ref, row_ref)
        for r in range(len(rows)):

            @pl.when(active[r])
            def _():
                for i, ref in enumerate(out_refs):
                    start = r * height + i * part
                    ref[r] = smooth[start : start + part]


def field_rows(ref, start, count, r, rows, radix):
    step = rows * radix
    return jnp.concatenate(
        [ref[pl.ds(start * step + t * rows + r, count, stride=step), :] for t in range(radix)], axis=1
    )


def first_kernel(
    rows, split, mask, state_ref, mix_ref, mask_hbm, table_hbm, row_hbm, *refs
):
    out_refs = refs[:split]
    load, weights_ref, mask_ref, table_ref, row_ref, sems = refs[split:]
    levels = mix_ref.shape[1]
    part = levels // split
    radix = out_refs[0].shape[2] // LANES
    span = levels * rows * radix
    me = lax.axis_index("lat")
    field = jnp.bitwise_xor(me // split, mask)
    core = lax.rem(me, split)
    copies = [
        pltpu.make_async_copy(state_ref.at[pl.ds(pl.multiple_of(field * span, span), span)], load, sems.at[0]),
        pltpu.make_async_copy(mix_ref.at[field], weights_ref, sems.at[1]),
        pltpu.make_async_copy(mask_hbm, mask_ref, sems.at[2]),
        pltpu.make_async_copy(row_hbm, row_ref, sems.at[3]),
        pltpu.make_async_copy(table_hbm, table_ref, sems.at[4]),
    ]
    for copy in copies:
        copy.start()
    copies[1].wait()
    copies[0].wait()
    weights = halves(
        jnp.concatenate(
            [
                weights_ref[pl.ds(pl.multiple_of(jnp.bitwise_xor(core, c) * part, part), part), :]
                for c in range(split)
            ],
            axis=0,
        )
    )
    for r in range(rows):
        mixed = split_product(weights, halves(field_rows(load, 0, levels, r, rows, radix)))
        for c in range(split):
            out_refs[c][r] = mixed[c * part : (c + 1) * part]
    copies[2].wait()
    copies[3].wait()
    filter_blocks([me * rows + r for r in range(rows)], out_refs, mask_ref, table_ref, row_ref, copies[4])


def first_blocks(view, vertical_mix, polar_mask, tables, lon, rows, split, mask):
    table, row_table = tables
    levels = vertical_mix.shape[1]
    part = levels // split
    hbm = pl.BlockSpec(memory_space=pltpu.HBM)
    return pl.pallas_call(
        functools.partial(first_kernel, rows, split, mask),
        out_shape=[jax.ShapeDtypeStruct((rows, part, lon), F32)] * split,
        in_specs=[hbm] * 5,
        out_specs=[pl.BlockSpec(memory_space=pltpu.VMEM)] * split,
        scratch_shapes=[
            pltpu.VMEM((levels * rows * lon // LANES, LANES), F32),
            pltpu.VMEM(vertical_mix.shape[1:], F32),
            pltpu.SMEM(polar_mask.shape, jnp.int32),
            pltpu.VMEM(table.shape, BF16),
            pltpu.VMEM(row_table.shape, F32),
            pltpu.SemaphoreType.DMA((5,)),
        ],
        compiler_params=pltpu.CompilerParams(vmem_limit_bytes=VMEM_LIMIT),
        name="first_blocks",
    )(view, vertical_mix, polar_mask, table, row_table)


def spread(values, groups, width, count):
    lane = lax.broadcasted_iota(jnp.int32, (width, width * count), 1)
    repeat = (lax.rem(lane, width) == lax.broadcasted_iota(jnp.int32, lane.shape, 0)).astype(BF16)
    lane_group = lax.broadcasted_iota(jnp.int32, (1, width * count), 1) // width
    keep = jnp.concatenate(
        [
            jnp.broadcast_to((lane_group == group).astype(F32), (height, width * count))
            for group, height in groups
        ],
        axis=0,
    )
    return [
        (jnp.dot(value, repeat, preferred_element_type=F32) * keep).astype(BF16) for value in halves(values)
    ]


def rest_kernel(
    rows,
    split,
    masks,
    own_hbm,
    *refs,
):
    sources = [own_hbm]
    if split > 1:
        sources.append(refs[0])
        refs = refs[1:]
    (mix_ref, mask_hbm, coupling_ref, fractions_ref, index_ref, table_hbm, row_hbm) = refs[:7]
    out_refs = refs[7 : 7 + len(masks)]
    flux_ref = refs[7 + len(masks)]
    load, mask_ref, table_ref, row_ref, sems = refs[8 + len(masks) :]
    fields, levels, _ = mix_ref.shape
    part = levels // split
    radix = out_refs[0].shape[2] // LANES
    me = lax.axis_index("lat")
    chip = me // split
    core = lax.rem(me, split)
    copies = [pltpu.make_async_copy(ref, load.at[i], sems.at[i]) for i, ref in enumerate(sources)]
    mask_copy = pltpu.make_async_copy(mask_hbm, mask_ref, sems.at[2])
    row_copy = pltpu.make_async_copy(row_hbm, row_ref, sems.at[3])
    table_copy = pltpu.make_async_copy(table_hbm, table_ref, sems.at[4])
    for copy in copies + [mask_copy, row_copy, table_copy]:
        copy.start()
    chosen = [jnp.bitwise_xor(chip, mask) if split > 1 else mask for mask in masks]
    level_start = pl.multiple_of(core * part, part)
    blocks = [mix_ref[field, pl.ds(level_start, part), :] for field in chosen]
    blocks += [mix_ref[f, levels - 1 : levels, :] for f in range(fields)]
    groups = [(field, part) for field in chosen] + [(f, 1) for f in range(fields)]
    high, low = (spread(jnp.concatenate(blocks, axis=0), groups, levels, fields))
    height = len(masks) * part
    for i, copy in enumerate(copies):
        copy.wait()
        for r in range(rows):
            right = halves(field_rows(load.at[i], 0, fields * levels, r, rows, radix))
            mixed = split_product((high, low), right)
            place = r if split == 1 else jnp.bitwise_xor(core, i) * rows + r
            for j, ref in enumerate(out_refs):
                ref[place] = mixed[j * part : (j + 1) * part]
            if i == 0:
                bottom = mixed[height:]
                speed = jnp.sqrt(bottom[0:1] * bottom[0:1] + bottom[1:2] * bottom[1:2] + 1.0)
                flux = split_product(halves(coupling_ref[...]), halves(bottom))
                flux_ref[r] = speed * flux * fractions_ref[pl.ds(index_ref[r], 1), :]
    mask_copy.wait()
    row_copy.wait()
    filter_blocks(
        [chip * split * rows + r for r in range(rows * split)],
        out_refs,
        mask_ref,
        table_ref,
        row_ref,
        table_copy,
    )


def rest_blocks(
    views, vertical_mix, polar_mask, coupling, fractions, weight_index, tables, lon, rows, masks
):
    split = len(views)
    table, row_table = tables
    levels = vertical_mix.shape[1]
    part = levels // split
    hbm = pl.BlockSpec(memory_space=pltpu.HBM)
    vmem = pl.BlockSpec(memory_space=pltpu.VMEM)
    smem = pl.BlockSpec(memory_space=pltpu.SMEM)
    *blocks, weighted = pl.pallas_call(
        functools.partial(rest_kernel, rows, split, masks),
        out_shape=[jax.ShapeDtypeStruct((rows * split, part, lon), F32)] * len(masks)
        + [jax.ShapeDtypeStruct((rows, coupling.shape[0], lon), F32)],
        in_specs=[hbm] * split + [vmem, hbm, vmem, vmem, smem, hbm, hbm],
        out_specs=[vmem] * (len(masks) + 1),
        scratch_shapes=[
            pltpu.VMEM((split,) + views[0].shape, F32),
            pltpu.SMEM(polar_mask.shape, jnp.int32),
            pltpu.VMEM(table.shape, BF16),
            pltpu.VMEM(row_table.shape, F32),
            pltpu.SemaphoreType.DMA((5,)),
        ],
        compiler_params=pltpu.CompilerParams(vmem_limit_bytes=VMEM_LIMIT),
        name="rest_blocks",
    )(*views, vertical_mix, polar_mask, coupling, fractions, weight_index, table, row_table)
    return blocks, weighted


def ocean_kernel(lat_count, bounds_ref, left_ref, own_ref, right_ref, out_ref):
    rows = own_ref.shape[0]
    slots = out_ref.shape[0]
    half = rows // 2
    me = lax.axis_index("lat")
    start = bounds_ref[me] - half
    length = bounds_ref[me + 1] - bounds_ref[me] + 2 * half + 1
    shift = start - (me - 1) * rows
    near = [ref[r] for ref in (left_ref, own_ref, right_ref) for r in range(rows)]
    for s in range(slots):
        row = start + s
        valid = (s < length) & (row >= 0) & (row < lat_count)
        picked = jnp.zeros_like(near[0])
        for p, value in enumerate(near):
            picked = jnp.where(valid & (shift + s == p), value, picked)
        out_ref[s] = picked


def ocean_slots(weighted, band_bounds, lat_count, device_count):
    rows, flux_count, lon = weighted.shape
    ends = device_count - 1
    left = lax.ppermute(weighted, "lat", [(i, i + 1) for i in range(ends)])
    right = lax.ppermute(weighted, "lat", [(i + 1, i) for i in range(ends)])
    vmem = pl.BlockSpec(memory_space=pltpu.VMEM)
    slots = pl.pallas_call(
        functools.partial(ocean_kernel, lat_count),
        out_shape=jax.ShapeDtypeStruct((3 * rows, flux_count, lon), F32),
        in_specs=[pl.BlockSpec(memory_space=pltpu.SMEM)] + [vmem] * 3,
        out_specs=vmem,
        name="ocean",
    )(band_bounds, left, weighted, right)
    return jnp.transpose(slots, (1, 0, 2))


def place_kernel(split, masks, direct, *refs):
    in_refs, out_ref, buffer, sems = refs[:-3], refs[-3], refs[-2], refs[-1]
    part, lon = in_refs[0].shape[1:]
    rows = in_refs[len(masks)].shape[0]
    radix = lon // LANES
    chip_rows = rows * split
    tile = radix * SUBLANES
    me = lax.axis_index("lat")
    chip = me // split
    core = lax.rem(me, split)
    group_span = out_ref.shape[0] // part

    def put(ref, index, row):
        start = row // SUBLANES * tile + lax.rem(row, SUBLANES)
        for t in range(radix):
            buffer[pl.ds(start + t * SUBLANES, part, stride=group_span), :] = ref[
                index, :, t * LANES : (t + 1) * LANES
            ]

    for i, mask in enumerate(masks):
        base = jnp.bitwise_xor(chip, mask) * chip_rows
        for r in range(chip_rows):
            put(in_refs[i], r, base + r)
    base = jnp.bitwise_xor(chip, direct) * chip_rows
    for c in range(split):
        for r in range(rows):
            put(in_refs[len(masks) + c], r, base + jnp.bitwise_xor(core, c) * rows + r)
    copy = pltpu.make_async_copy(buffer, out_ref, sems.at[0])
    copy.start()
    copy.wait()


def place(bundles, masks, direct_blocks, direct, lat_count):
    part, lon = bundles[0].shape[1:]
    size = part * lat_count * lon // LANES
    vmem = pl.BlockSpec(memory_space=pltpu.VMEM)
    out = pl.pallas_call(
        functools.partial(place_kernel, len(direct_blocks), masks, direct),
        out_shape=jax.ShapeDtypeStruct((size, LANES), F32),
        in_specs=[vmem] * (len(bundles) + len(direct_blocks)),
        out_specs=pl.BlockSpec(memory_space=pltpu.HBM),
        scratch_shapes=[pltpu.VMEM((size, LANES), F32), pltpu.SemaphoreType.DMA((1,))],
        compiler_params=pltpu.CompilerParams(vmem_limit_bytes=VMEM_LIMIT),
        name="place",
    )(*bundles, *direct_blocks)
    tiles = out.reshape(part, lat_count // SUBLANES, lon // LANES, SUBLANES, LANES)
    return tiles.transpose(0, 1, 3, 2, 4).reshape(part, lat_count, lon)


def body(device_count, state, vertical_mix, coupling, fractions, weight_index, band_bounds, polar_mask):
    field_count, level_count = vertical_mix.shape[:2]
    stack_count, row_count, lon_count = state.shape
    lat_count = polar_mask.shape[0]
    part = stack_count // device_count
    tables = transform_tables(lon_count, lat_count)
    radix = lon_count // LANES
    view = state.reshape(stack_count, row_count, radix, LANES).transpose(0, 2, 1, 3).reshape(-1, LANES)
    surface = (coupling, fractions, weight_index, tables, lon_count, row_count)

    def exchange(block, mask):
        return lax.ppermute(block, "lat", [(i, i ^ mask) for i in range(device_count)])

    if part == SUBLANES and level_count == 2 * part and field_count == len(BUNDLES) + 2:
        split = 2
        sibling = exchange(view, 1)
        near, far = first_blocks(
            view, vertical_mix, polar_mask, tables, lon_count, row_count, split, DIRECT
        )
        direct = [exchange(near, DIRECT * split), exchange(far, DIRECT * split + 1)]
        masks = BUNDLES + (0,)
        blocks, weighted = rest_blocks((view, sibling), vertical_mix, polar_mask, *surface, masks)
        moved = [exchange(block, mask * split) for block, mask in zip(blocks, BUNDLES)]
        state_out = place(moved + [blocks[-1]], masks, direct, DIRECT, lat_count)
    else:
        masks = tuple(range(field_count))
        blocks, weighted = rest_blocks((view,), vertical_mix, polar_mask, *surface, masks)
        stacked = jnp.concatenate(blocks, axis=1)
        moved = lax.all_to_all(stacked, "lat", split_axis=1, concat_axis=0, tiled=True)
        state_out = jnp.transpose(moved, (1, 0, 2))
    ocean = ocean_slots(weighted, band_bounds, lat_count, device_count)
    return (state_out, ocean)


def solution(mesh):
    return jax.shard_map(
        functools.partial(body, mesh.shape["lat"]),
        mesh=mesh,
        in_specs=(P("member", "lat", None), P(), P(), P(), P(("member", "lat")), P(), P()),
        out_specs=(P(("member", "lat"), None, None), P(None, ("member", "lat"), None)),
        check_vma=False,
    )
```

```python
import functools

import jax
import jax.numpy as jnp
import numpy as np
from jax import lax
from jax.experimental import pallas as pl
from jax.experimental.layout import Layout, with_layout_constraint
from jax.experimental.pallas import tpu as pltpu
from jax.sharding import PartitionSpec as P

COSCUT = 0.5
LANES = 128
SUBLANES = 8
DIRECT = (6,)
BUNDLES = (5, 7, 3, 4, 1, 2)
F32 = jnp.float32
BF16 = jnp.bfloat16
NORMAL = (((1,), (0,)), ((), ()))
TRANSPOSED = (((1,), (1,)), ((), ()))
VMEM_LIMIT = 48 << 20


def halves(values):
    high = values.astype(BF16)
    return high, (values - high.astype(F32)).astype(BF16)


def split_product(left, right, dims=NORMAL):
    dot = functools.partial(lax.dot_general, dimension_numbers=dims, preferred_element_type=F32)
    return dot(left[0], right[0]) + (dot(left[0], right[1]) + dot(left[1], right[0]))


def np_halves(values):
    values = np.asarray(values, np.float32)
    high = values.astype(jnp.bfloat16)
    return np.stack([high, (values - high.astype(np.float32)).astype(jnp.bfloat16)])


def transform_tables(lon_count, lat_count):
    radix = lon_count // LANES
    steps = radix // 2
    b = np.arange(LANES)[:, None]
    k2 = np.arange(LANES)[None, :]
    table = np.zeros((steps * 2 * LANES + LANES, 2 * LANES))
    for k in range(1, steps + 1):
        angle = 2 * np.pi * ((b * (k + radix * k2)) % lon_count) / lon_count
        c, s = np.cos(angle), np.sin(angle)
        table[(k - 1) * 2 * LANES : k * 2 * LANES] = np.block([[c, -s], [s, c]])
    half = LANES // 2
    angle = 2 * np.pi * ((b * k2) % LANES) / LANES
    table[steps * 2 * LANES :, :LANES] = np.concatenate(
        [np.cos(angle[:, : half + 1]), np.sin(angle[:, 1:half])], axis=1
    )
    wave = np.zeros((steps + 1, 2 * LANES))
    scale = np.full((steps + 1, 2 * LANES), 2.0 / lon_count)
    wave[0, :LANES] = np.concatenate([np.arange(half + 1), np.arange(1, half)]) * radix
    scale[0, [0, half]] = 1.0 / lon_count
    for k in range(1, steps + 1):
        wave[k] = np.tile(k + radix * np.arange(LANES), 2)
    limit = COSCUT**2 * np.sin(np.pi * wave / lon_count) ** 2
    latitude = np.pi * ((np.arange(lat_count) + 0.5) / lat_count - 0.5)
    square = np.repeat(np.cos(latitude)[:, None] ** 2, 2 * LANES, axis=1)
    rows = np.concatenate([limit, scale, square])
    rows = np.pad(rows, ((0, -len(rows) % SUBLANES), (0, 0)))
    return np_halves(table), rows.astype(np.float32)


def filtered(fields, squares, table_ref, row_ref):
    radix = fields.shape[1] // LANES
    half = radix // 2
    height = fields.shape[0] // len(squares)
    parts = [fields[:, a * LANES : (a + 1) * LANES] for a in range(radix)]
    sums = [parts[a] + parts[radix - a] for a in range(1, half + 1)]
    gaps = [parts[a] - parts[radix - a] for a in range(1, half + 1)]

    def pair(k):
        if k == 0:
            rows, width = slice(half * 2 * LANES, half * 2 * LANES + LANES), LANES
        else:
            rows, width = slice((k - 1) * 2 * LANES, k * 2 * LANES), 2 * LANES
        return table_ref[0, rows, :width], table_ref[1, rows, :width]

    def gain(k, width):
        limit = row_ref[k : k + 1, :LANES]
        scale = row_ref[half + 1 + k : half + 2 + k, :LANES]
        groups = [
            jnp.broadcast_to(square / jnp.maximum(square, limit) * scale, (height, LANES))
            for square in squares
        ]
        groups = jnp.concatenate(groups, axis=0)
        return groups if width == LANES else jnp.concatenate([groups, groups], axis=1)

    total = parts[0]
    for value in sums:
        total = total + value
    spectrum = split_product(halves(total), pair(0)) * gain(0, LANES)
    base = split_product(halves(spectrum), pair(0), TRANSPOSED)
    cosines, sines = [], []
    for k in range(1, half + 1):
        real, imag = parts[0], None
        for a in range(1, half + 1):
            angle = 2 * np.pi * (a * k % radix) / radix
            real = real + float(np.cos(angle)) * sums[a - 1]
            term = float(-np.sin(angle)) * gaps[a - 1]
            imag = term if imag is None else imag + term
        both = jnp.concatenate([real, imag], axis=1)
        spectrum = split_product(halves(both), pair(k)) * gain(k, 2 * LANES)
        series = split_product(halves(spectrum), pair(k), TRANSPOSED)
        cosines.append(series[:, :LANES])
        sines.append(series[:, LANES:])
    whole = base
    for value in cosines:
        whole = whole + value
    lower, upper = [], []
    for a in range(1, half + 1):
        even, odd = base, None
        for k in range(1, half + 1):
            angle = 2 * np.pi * (a * k % radix) / radix
            even = even + float(np.cos(angle)) * cosines[k - 1]
            term = float(np.sin(angle)) * sines[k - 1]
            odd = term if odd is None else odd + term
        lower.append(even - odd)
        upper.append(even + odd)
    return jnp.concatenate([whole] + lower + upper[::-1], axis=1)


def filter_blocks(rows, out_refs, mask_ref, table_ref, row_ref):
    part = out_refs[0].shape[1]
    height = len(out_refs) * part
    radix = out_refs[0].shape[2] // LANES
    first_square = 2 * (radix // 2 + 1)
    active = [mask_ref[row] == 1 for row in rows]

    @pl.when(functools.reduce(jnp.logical_or, active))
    def _():
        fields = jnp.concatenate([ref[r] for r in range(len(rows)) for ref in out_refs], axis=0)
        squares = [row_ref[pl.ds(first_square + row, 1), :][:, :LANES] for row in rows]
        smooth = filtered(fields, squares, table_ref, row_ref)
        for r in range(len(rows)):

            @pl.when(active[r])
            def _():
                for i, ref in enumerate(out_refs):
                    start = r * height + i * part
                    ref[r] = smooth[start : start + part]


def field_rows(ref, start, count, r, rows, radix):
    step = rows * radix
    return jnp.concatenate(
        [ref[pl.ds(start * step + t * rows + r, count, stride=step), :] for t in range(radix)], axis=1
    )


def first_kernel(rows, split, masks, state_ref, mix_ref, mask_hbm, table_hbm, row_hbm, *refs):
    outs = split * len(masks)
    out_refs = refs[:outs]
    load, weights_ref, mask_ref, table_ref, row_ref, sems = refs[outs:]
    levels = mix_ref.shape[1]
    part = levels // split
    radix = out_refs[0].shape[2] // LANES
    span = levels * rows * radix
    me = lax.axis_index("lat")
    core = lax.rem(me, split)
    fields = [jnp.bitwise_xor(me // split, mask) for mask in masks]
    loads = [
        pltpu.make_async_copy(
            state_ref.at[pl.ds(pl.multiple_of(field * span, span), span)], load.at[i], sems.at[4 + i]
        )
        for i, field in enumerate(fields)
    ]
    others = [
        pltpu.make_async_copy(mix_ref, weights_ref, sems.at[0]),
        pltpu.make_async_copy(mask_hbm, mask_ref, sems.at[1]),
        pltpu.make_async_copy(row_hbm, row_ref, sems.at[2]),
        pltpu.make_async_copy(table_hbm, table_ref, sems.at[3]),
    ]
    for copy in loads + others:
        copy.start()
    others[0].wait()
    for i, field in enumerate(fields):
        starts = [pl.multiple_of(jnp.bitwise_xor(core, c) * part, part) for c in range(split)]
        weights = halves(
            jnp.concatenate([weights_ref[field, pl.ds(start, part), :] for start in starts], axis=0)
        )
        loads[i].wait()
        for r in range(rows):
            mixed = split_product(weights, halves(field_rows(load.at[i], 0, levels, r, rows, radix)))
            for c in range(split):
                out_refs[i * split + c][r] = mixed[c * part : (c + 1) * part]
    others[1].wait()
    others[2].wait()
    others[3].wait()
    filter_blocks([me * rows + r for r in range(rows)], out_refs, mask_ref, table_ref, row_ref)


def first_blocks(view, vertical_mix, polar_mask, tables, lon, rows, split, masks):
    table, row_table = tables
    levels = vertical_mix.shape[1]
    part = levels // split
    operands = [
        pltpu.with_memory_space_constraint(value, pltpu.HBM)
        for value in (view, vertical_mix, polar_mask, jnp.asarray(table), jnp.asarray(row_table))
    ]
    return pl.pallas_call(
        functools.partial(first_kernel, rows, split, masks),
        out_shape=[pltpu.VMEM((rows, part, lon), F32)] * (split * len(masks)),
        in_specs=[pl.BlockSpec(memory_space=pltpu.HBM)] * len(operands),
        out_specs=[pl.BlockSpec(memory_space=pltpu.VMEM)] * (split * len(masks)),
        scratch_shapes=[
            pltpu.VMEM((len(masks), levels * rows * lon // LANES, LANES), F32),
            pltpu.VMEM(vertical_mix.shape, F32),
            pltpu.SMEM(polar_mask.shape, jnp.int32),
            pltpu.VMEM(table.shape, BF16),
            pltpu.VMEM(row_table.shape, F32),
            pltpu.SemaphoreType.DMA((4 + len(masks),)),
        ],
        compiler_params=pltpu.CompilerParams(vmem_limit_bytes=VMEM_LIMIT),
        name="first_blocks",
    )(*operands)


def spread(values, groups, width, count):
    lane = lax.broadcasted_iota(jnp.int32, (width, width * count), 1)
    repeat = (lax.rem(lane, width) == lax.broadcasted_iota(jnp.int32, lane.shape, 0)).astype(BF16)
    lane_group = lax.broadcasted_iota(jnp.int32, (1, width * count), 1) // width
    keep = jnp.concatenate(
        [
            jnp.broadcast_to((lane_group == group).astype(F32), (height, width * count))
            for group, height in groups
        ],
        axis=0,
    )
    return [
        (jnp.dot(value, repeat, preferred_element_type=F32) * keep).astype(BF16) for value in halves(values)
    ]


def rest_kernel(rows, split, masks, *refs):
    sources = refs[:split]
    refs = refs[split:] if split == 1 else refs[split + 1 :]
    (mix_ref, mask_ref, coupling_ref, fractions_ref, index_ref, table_ref, row_ref) = refs[:7]
    out_refs = refs[7 : 7 + len(masks)]
    flux_ref = refs[7 + len(masks)]
    fields, levels, _ = mix_ref.shape
    part = levels // split
    radix = out_refs[0].shape[2] // LANES
    me = lax.axis_index("lat")
    chip = me // split
    core = lax.rem(me, split)
    chosen = [jnp.bitwise_xor(chip, mask) if split > 1 else mask for mask in masks]
    level_start = pl.multiple_of(core * part, part)
    blocks = [mix_ref[field, pl.ds(level_start, part), :] for field in chosen]
    blocks += [mix_ref[f, levels - 1 : levels, :] for f in range(fields)]
    groups = [(field, part) for field in chosen] + [(f, 1) for f in range(fields)]
    weights = spread(jnp.concatenate(blocks, axis=0), groups, levels, fields)
    height = len(masks) * part
    for i, source in enumerate(sources):
        for r in range(rows):
            right = halves(field_rows(source, 0, fields * levels, r, rows, radix))
            mixed = split_product(weights, right)
            place = r if split == 1 else jnp.bitwise_xor(core, i) * rows + r
            for j, ref in enumerate(out_refs):
                ref[place] = mixed[j * part : (j + 1) * part]
            if i == 0:
                bottom = mixed[height:]
                speed = jnp.sqrt(bottom[0:1] * bottom[0:1] + bottom[1:2] * bottom[1:2] + 1.0)
                flux = split_product(halves(coupling_ref[...]), halves(bottom))
                flux_ref[r] = speed * flux * fractions_ref[pl.ds(index_ref[r], 1), :]
    filter_blocks(
        [chip * split * rows + r for r in range(rows * split)], out_refs, mask_ref, table_ref, row_ref
    )


def rest_blocks(
    views, after, vertical_mix, polar_mask, coupling, fractions, weight_index, tables, lon, rows, masks
):
    split = len(views)
    levels = vertical_mix.shape[1]
    part = levels // split
    vmem = pl.BlockSpec(memory_space=pltpu.VMEM)
    smem = pl.BlockSpec(memory_space=pltpu.SMEM)
    *blocks, weighted = pl.pallas_call(
        functools.partial(rest_kernel, rows, split, masks),
        out_shape=[pltpu.VMEM((rows * split, part, lon), F32)] * len(masks)
        + [pltpu.VMEM((rows, coupling.shape[0], lon), F32)],
        in_specs=[vmem] * split
        + [vmem] * len(after)
        + [vmem, smem, vmem, vmem, smem, vmem, vmem],
        out_specs=[vmem] * (len(masks) + 1),
        compiler_params=pltpu.CompilerParams(vmem_limit_bytes=VMEM_LIMIT),
        name="rest_blocks",
    )(*views, *after, vertical_mix, polar_mask, coupling, fractions, weight_index, *tables)
    return blocks, weighted


def ocean_kernel(lat_count, split, bounds_ref, own_ref, *refs):
    near_refs, out_ref = refs[:-1], refs[-1]
    rows = own_ref.shape[0]
    slots = out_ref.shape[0]
    half = rows // 2
    me = lax.axis_index("lat")
    start = bounds_ref[me] - half
    length = bounds_ref[me + 1] - bounds_ref[me] + 2 * half + 1
    shift = start - (me - 1) * rows
    first, last = ([ref[r] for r in range(rows)] for ref in near_refs)
    if split > 1:
        upper = lax.rem(me, split) == 0
        first, last = (
            [jnp.where(upper, outer, other) for outer, other in zip(last, first)],
            [jnp.where(upper, other, outer) for outer, other in zip(last, first)],
        )
    near = first + [own_ref[r] for r in range(rows)] + last
    for s in range(slots):
        row = start + s
        valid = (s < length) & (row >= 0) & (row < lat_count)
        picked = jnp.zeros_like(near[0])
        for p, value in enumerate(near):
            picked = jnp.where(valid & (shift + s == p), value, picked)
        out_ref[s] = picked


def ocean_slots(weighted, band_bounds, lat_count, device_count, split):
    rows, flux_count, lon = weighted.shape
    ends = device_count - 1
    if split == 2:
        pairs = [(i, i + 1) for i in range(1, ends, 2)]
        near = [
            lax.ppermute(weighted, "lat", [(i, i ^ 1) for i in range(device_count)]),
            lax.ppermute(weighted, "lat", pairs + [(j, i) for i, j in pairs]),
        ]
    else:
        near = [
            lax.ppermute(weighted, "lat", [(i, i + 1) for i in range(ends)]),
            lax.ppermute(weighted, "lat", [(i + 1, i) for i in range(ends)]),
        ]
    vmem = pl.BlockSpec(memory_space=pltpu.VMEM)
    slots = pl.pallas_call(
        functools.partial(ocean_kernel, lat_count, split),
        out_shape=jax.ShapeDtypeStruct((3 * rows, flux_count, lon), F32),
        in_specs=[pl.BlockSpec(memory_space=pltpu.SMEM)] + [vmem] * 3,
        out_specs=vmem,
        name="ocean",
    )(band_bounds, weighted, *near)
    return slots


def place_kernel(split, masks, direct, *refs):
    blocks = len(masks) + split * len(direct)
    in_refs, (out_ref, buffer, sems) = refs[:blocks], refs[-3:]
    part, lon = in_refs[0].shape[1:]
    rows = in_refs[len(masks)].shape[0]
    radix = lon // LANES
    chip_rows = rows * split
    tile = radix * SUBLANES
    span = out_ref.shape[0] // part
    chips = SUBLANES // chip_rows
    me = lax.axis_index("lat")
    chip = me // split
    core = lax.rem(me, split)
    copies = []
    for group in range(span // tile):
        for low in range(chips):
            mask = group * chips + low
            base = jnp.bitwise_xor(lax.rem(chip, chips), low) * chip_rows
            if mask in masks:
                ref = in_refs[masks.index(mask)]
                items = [(ref, r, base + r) for r in range(chip_rows)]
            else:
                first = len(masks) + direct.index(mask) * split
                items = [
                    (in_refs[first + c], r, base + jnp.bitwise_xor(core, c) * rows + r)
                    for c in range(split)
                    for r in range(rows)
                ]
            for ref, index, row in items:
                for t in range(radix):
                    buffer[group, pl.ds(row + t * SUBLANES, part, stride=tile), :] = ref[
                        index, :, t * LANES : (t + 1) * LANES
                    ]
        start = jnp.bitwise_xor(chip // chips, group) * tile
        for f in range(part):
            copy = pltpu.make_async_copy(
                buffer.at[group, pl.ds(f * tile, tile)],
                out_ref.at[pl.ds(pl.multiple_of(f * span + start, SUBLANES), tile)],
                sems.at[group, f],
            )
            copy.start()
            copies.append(copy)
    for copy in copies:
        copy.wait()


def place(bundles, masks, direct_blocks, direct, lat_count, after):
    part, lon = bundles[0].shape[1:]
    rows = direct_blocks[0].shape[0]
    split = len(direct_blocks) // len(direct)
    size = part * lat_count * lon // LANES
    groups = lat_count // SUBLANES
    vmem = pl.BlockSpec(memory_space=pltpu.VMEM)
    out = pl.pallas_call(
        functools.partial(place_kernel, split, masks, direct),
        out_shape=jax.ShapeDtypeStruct((size, LANES), F32),
        in_specs=[vmem] * (len(bundles) + len(direct_blocks)) + [pl.BlockSpec(memory_space=pl.ANY)],
        out_specs=pl.BlockSpec(memory_space=pltpu.HBM),
        scratch_shapes=[
            pltpu.VMEM((groups, size // groups, LANES), F32),
            pltpu.SemaphoreType.DMA((groups, part)),
        ],
        compiler_params=pltpu.CompilerParams(vmem_limit_bytes=VMEM_LIMIT),
        name="place",
    )(*bundles, *direct_blocks, after)
    tiles = out.reshape(part, groups, lon // LANES, SUBLANES, LANES)
    return tiles.transpose(0, 1, 3, 2, 4).reshape(part, lat_count, lon)


def body(device_count, state, vertical_mix, coupling, fractions, weight_index, band_bounds, polar_mask):
    field_count, level_count = vertical_mix.shape[:2]
    stack_count, row_count, lon_count = state.shape
    lat_count = polar_mask.shape[0]
    part = stack_count // device_count
    tables = transform_tables(lon_count, lat_count)
    radix = lon_count // LANES
    blocked = with_layout_constraint(
        state.reshape(stack_count, row_count, radix, LANES), Layout(major_to_minor=(0, 2, 1, 3))
    )
    view = blocked.transpose(0, 2, 1, 3).reshape(-1, LANES)
    surface = (coupling, fractions, weight_index, tables, lon_count, row_count)

    def exchange(block, mask):
        return lax.ppermute(block, "lat", [(i, i ^ mask) for i in range(device_count)])

    if part == SUBLANES and level_count == 2 * part and field_count == len(BUNDLES) + len(DIRECT) + 1:
        split = 2
        sibling = exchange(view, 1)
        first = first_blocks(
            view, vertical_mix, polar_mask, tables, lon_count, row_count, split, DIRECT
        )
        partners = [mask * split + c for mask in DIRECT for c in range(split)]
        direct = [exchange(block, partner) for block, partner in zip(first, partners)]
        masks = BUNDLES + (0,)
        blocks, weighted = rest_blocks((view, sibling), first[:1], vertical_mix, polar_mask, *surface, masks)
        (blocks[0], *direct) = lax.optimization_barrier((blocks[0], *direct))
        moved = [exchange(block, mask * split) for block, mask in zip(blocks, BUNDLES)]
        ocean = ocean_slots(weighted, band_bounds, lat_count, device_count, split)
        state_out = place(moved + [blocks[-1]], masks, direct, DIRECT, lat_count, ocean)
    else:
        masks = tuple(range(field_count))
        blocks, weighted = rest_blocks((view,), (), vertical_mix, polar_mask, *surface, masks)
        stacked = jnp.concatenate(blocks, axis=1)
        moved = lax.all_to_all(stacked, "lat", split_axis=1, concat_axis=0, tiled=True)
        state_out = jnp.transpose(moved, (1, 0, 2))
        ocean = ocean_slots(weighted, band_bounds, lat_count, device_count, 1)
    return (state_out, jnp.transpose(ocean, (1, 0, 2)))


def solution(mesh):
    return jax.shard_map(
        functools.partial(body, mesh.shape["lat"]),
        mesh=mesh,
        in_specs=(P("member", "lat", None), P(), P(), P(), P(("member", "lat")), P(), P()),
        out_specs=(P(("member", "lat"), None, None), P(None, ("member", "lat"), None)),
        check_vma=False,
    )
```

```python
import functools

import jax
import jax.numpy as jnp
import numpy as np
from jax import lax
from jax.experimental import pallas as pl
from jax.experimental.layout import Layout, with_layout_constraint
from jax.experimental.pallas import tpu as pltpu
from jax.sharding import PartitionSpec as P

COSCUT = 0.5
LANES = 128
SUBLANES = 8
STEPS = ((4, 4), (7, 7), (3, 3), (5, 5), (1, 1), (6, 6), (2, 2))
RAW_STEPS = 1
RAW_TIE = 2
HALO_STEP = 9
HALO_SWAP = 0
SWAPS = ((0, 1, 2, 7), (3, 4, 5, 6))
F32 = jnp.float32
BF16 = jnp.bfloat16
NORMAL = (((1,), (0,)), ((), ()))
TRANSPOSED = (((1,), (1,)), ((), ()))
VMEM_LIMIT = 32 << 20
SMALL_LIMIT = 8 << 20


def halves(values):
    high = values.astype(BF16)
    return high, (values - high.astype(F32)).astype(BF16)


def split_product(left, right, dims=NORMAL):
    dot = functools.partial(lax.dot_general, dimension_numbers=dims, preferred_element_type=F32)
    return dot(left[0], right[0]) + (dot(left[0], right[1]) + dot(left[1], right[0]))


def np_halves(values):
    values = np.asarray(values, np.float32)
    high = values.astype(jnp.bfloat16)
    return np.stack([high, (values - high.astype(np.float32)).astype(jnp.bfloat16)])


def transform_tables(lon_count, lat_count):
    radix = lon_count // LANES
    steps = radix // 2
    b = np.arange(LANES)[:, None]
    k2 = np.arange(LANES)[None, :]
    table = np.zeros((steps * 2 * LANES + LANES, 2 * LANES))
    for k in range(1, steps + 1):
        angle = 2 * np.pi * ((b * (k + radix * k2)) % lon_count) / lon_count
        c, s = np.cos(angle), np.sin(angle)
        table[(k - 1) * 2 * LANES : k * 2 * LANES] = np.block([[c, -s], [s, c]])
    half = LANES // 2
    angle = 2 * np.pi * ((b * k2) % LANES) / LANES
    table[steps * 2 * LANES :, :LANES] = np.concatenate(
        [np.cos(angle[:, : half + 1]), np.sin(angle[:, 1:half])], axis=1
    )
    wave = np.zeros((steps + 1, 2 * LANES))
    scale = np.full((steps + 1, 2 * LANES), 2.0 / lon_count)
    wave[0, :LANES] = np.concatenate([np.arange(half + 1), np.arange(1, half)]) * radix
    scale[0, [0, half]] = 1.0 / lon_count
    for k in range(1, steps + 1):
        wave[k] = np.tile(k + radix * np.arange(LANES), 2)
    limit = COSCUT**2 * np.sin(np.pi * wave / lon_count) ** 2
    latitude = np.pi * ((np.arange(lat_count) + 0.5) / lat_count - 0.5)
    square = np.repeat(np.cos(latitude)[:, None] ** 2, 2 * LANES, axis=1)
    rows = np.concatenate([limit, scale, square])
    rows = np.pad(rows, ((0, -len(rows) % SUBLANES), (0, 0)))
    return np_halves(table), rows.astype(np.float32)


def filtered(fields, squares, table_ref, row_ref):
    radix = fields.shape[1] // LANES
    half = radix // 2
    height = fields.shape[0] // len(squares)
    parts = [fields[:, a * LANES : (a + 1) * LANES] for a in range(radix)]
    sums = [parts[a] + parts[radix - a] for a in range(1, half + 1)]
    gaps = [parts[a] - parts[radix - a] for a in range(1, half + 1)]

    def pair(k):
        if k == 0:
            rows, width = slice(half * 2 * LANES, half * 2 * LANES + LANES), LANES
        else:
            rows, width = slice((k - 1) * 2 * LANES, k * 2 * LANES), 2 * LANES
        return table_ref[0, rows, :width], table_ref[1, rows, :width]

    def gain(k, width):
        limit = row_ref[k : k + 1, :LANES]
        scale = row_ref[half + 1 + k : half + 2 + k, :LANES]
        groups = [
            jnp.broadcast_to(square / jnp.maximum(square, limit) * scale, (height, LANES))
            for square in squares
        ]
        groups = jnp.concatenate(groups, axis=0)
        return groups if width == LANES else jnp.concatenate([groups, groups], axis=1)

    total = parts[0]
    for value in sums:
        total = total + value
    spectrum = split_product(halves(total), pair(0)) * gain(0, LANES)
    base = split_product(halves(spectrum), pair(0), TRANSPOSED)
    cosines, sines = [], []
    for k in range(1, half + 1):
        real, imag = parts[0], None
        for a in range(1, half + 1):
            angle = 2 * np.pi * (a * k % radix) / radix
            real = real + float(np.cos(angle)) * sums[a - 1]
            term = float(-np.sin(angle)) * gaps[a - 1]
            imag = term if imag is None else imag + term
        both = jnp.concatenate([real, imag], axis=1)
        spectrum = split_product(halves(both), pair(k)) * gain(k, 2 * LANES)
        series = split_product(halves(spectrum), pair(k), TRANSPOSED)
        cosines.append(series[:, :LANES])
        sines.append(series[:, LANES:])
    whole = base
    for value in cosines:
        whole = whole + value
    lower, upper = [], []
    for a in range(1, half + 1):
        even, odd = base, None
        for k in range(1, half + 1):
            angle = 2 * np.pi * (a * k % radix) / radix
            even = even + float(np.cos(angle)) * cosines[k - 1]
            term = float(np.sin(angle)) * sines[k - 1]
            odd = term if odd is None else odd + term
        lower.append(even - odd)
        upper.append(even + odd)
    return jnp.concatenate([whole] + lower + upper[::-1], axis=1)


def filter_blocks(rows, out_refs, mask_ref, table_ref, row_ref):
    part = out_refs[0].shape[1]
    height = len(out_refs) * part
    radix = out_refs[0].shape[2] // LANES
    first_square = 2 * (radix // 2 + 1)
    active = [mask_ref[row] == 1 for row in rows]

    @pl.when(functools.reduce(jnp.logical_or, active))
    def _():
        fields = jnp.concatenate([ref[r] for r in range(len(rows)) for ref in out_refs], axis=0)
        squares = [row_ref[pl.ds(first_square + row, 1), :][:, :LANES] for row in rows]
        smooth = filtered(fields, squares, table_ref, row_ref)
        for r in range(len(rows)):

            @pl.when(active[r])
            def _():
                for i, ref in enumerate(out_refs):
                    start = r * height + i * part
                    ref[r] = smooth[start : start + part]


def step_mask(chip, step):
    first, second = STEPS[step] if step < len(STEPS) else (0, 0)
    if first == second:
        return first
    if isinstance(chip, int):
        return first if (chip >> 2 ^ chip >> 1) & 1 else second
    return jnp.where(lax.rem(chip // 4 + chip // 2, 2) == 1, first, second)


def field_rows(ref, start, count, r, rows, radix):
    step = rows * radix
    return jnp.concatenate(
        [ref[pl.ds(start * step + t * rows + r, count, stride=step), :] for t in range(radix)], axis=1
    )


def spread(values, groups, width, count):
    lane = lax.broadcasted_iota(jnp.int32, (width, width * count), 1)
    repeat = (lax.rem(lane, width) == lax.broadcasted_iota(jnp.int32, lane.shape, 0)).astype(BF16)
    lane_group = lax.broadcasted_iota(jnp.int32, (1, width * count), 1) // width
    keep = jnp.concatenate(
        [
            jnp.broadcast_to((lane_group == group).astype(F32), (height, width * count))
            for group, height in groups
        ],
        axis=0,
    )
    return [
        (jnp.dot(value, repeat, preferred_element_type=F32) * keep).astype(BF16) for value in halves(values)
    ]


def mix_kernel(rows, split, first, steps, *refs):
    outs = steps + split if split > 1 else steps
    inputs, refs = refs[:8], refs[8:]
    out_refs, flux_ref, refs = refs[:outs], refs[outs], refs[outs + 1 :]
    (load, mix_ref, mask_ref, coupling_ref, fractions_ref, index_ref, table_ref, row_ref, sems) = refs
    copies = [
        pltpu.make_async_copy(source, target, sems.at[i])
        for i, (source, target) in enumerate(zip(inputs, refs[:-1]))
    ]
    for copy in copies:
        copy.start()
    fields, levels, _ = mix_ref.shape
    part = levels // split
    lon = flux_ref.shape[2]
    radix = lon // LANES
    me = lax.axis_index("lat")
    core = lax.rem(me, split)
    blocks = list(out_refs)
    if split > 1:
        blocks = [ref.at[c] for ref in out_refs[:steps] for c in range(split)] + blocks[steps:]
    chosen, weights = [], []
    copies[1].wait()
    for step in range(first, fields):
        field = jnp.bitwise_xor(me // split, step_mask(me // split, step)) if split > 1 else step
        for c in range(split):
            start = pl.multiple_of(jnp.bitwise_xor(core, c) * part, part) if split > 1 else 0
            weights.append(mix_ref[field, pl.ds(start, part), :])
            chosen.append((field, part))
    weights += [mix_ref[f, levels - 1 : levels, :] for f in range(fields)]
    chosen += [(f, 1) for f in range(fields)]
    left = spread(jnp.concatenate(weights, axis=0), chosen, levels, fields)
    copies[0].wait()
    bottoms = []
    for r in range(rows):
        mixed = split_product(left, halves(field_rows(load, 0, fields * levels, r, rows, radix)))
        for j, ref in enumerate(blocks):
            ref[r] = mixed[j * part : (j + 1) * part]
        bottoms.append(mixed[len(blocks) * part :])
    for copy in copies[2:]:
        copy.wait()
    for r, bottom in enumerate(bottoms):
        speed = jnp.sqrt(bottom[0:1] * bottom[0:1] + bottom[1:2] * bottom[1:2] + 1.0)
        flux = split_product(halves(coupling_ref[...]), halves(bottom))
        flux_ref[r] = speed * flux * fractions_ref[pl.ds(index_ref[r], 1), :]
    filter_blocks([me * rows + r for r in range(rows)], blocks, mask_ref, table_ref, row_ref)


def mixed_blocks(
    view, vertical_mix, polar_mask, coupling, fractions, weight_index, tables, lon, rows, split, first, steps
):
    part = vertical_mix.shape[1] // split
    arrays = (view, vertical_mix, polar_mask, coupling, fractions, weight_index) + tuple(
        jnp.asarray(table) for table in tables
    )
    operands = [pltpu.with_memory_space_constraint(value, pltpu.HBM) for value in arrays]
    spaces = [pltpu.SMEM if value.dtype == jnp.int32 else pltpu.VMEM for value in arrays]
    block = (rows, part, lon)
    outs = [pltpu.VMEM((split,) + block if split > 1 else block, F32)] * steps
    outs += [pltpu.VMEM(block, F32)] * (split if split > 1 else 0)
    outs += [pltpu.VMEM((rows, coupling.shape[0], lon), F32)]
    return pl.pallas_call(
        functools.partial(mix_kernel, rows, split, first, steps),
        out_shape=outs,
        in_specs=[pl.BlockSpec(memory_space=pltpu.HBM)] * len(operands),
        out_specs=[pl.BlockSpec(memory_space=pltpu.VMEM)] * len(outs),
        scratch_shapes=[space(value.shape, value.dtype) for space, value in zip(spaces, arrays)]
        + [pltpu.SemaphoreType.DMA((len(arrays),))],
        compiler_params=pltpu.CompilerParams(vmem_limit_bytes=VMEM_LIMIT),
        name="mixed_blocks",
    )(*operands)


def pick_kernel(split, steps, view_ref, *refs):
    out_refs, sems = refs[:-1], refs[-1]
    span = out_refs[0].shape[0]
    chip = lax.axis_index("lat") // split
    copies = []
    for i, step in enumerate(steps):
        start = pl.multiple_of(jnp.bitwise_xor(chip, step_mask(chip, step)) * span, span)
        copies.append(pltpu.make_async_copy(view_ref.at[pl.ds(start, span)], out_refs[i], sems.at[i]))
        copies[-1].start()
    for copy in copies:
        copy.wait()


def raw_fields(view, field_count, split, steps):
    shape = (view.shape[0] // field_count, LANES)
    return pl.pallas_call(
        functools.partial(pick_kernel, split, steps),
        out_shape=[pltpu.VMEM(shape, F32)] * len(steps),
        in_specs=[pl.BlockSpec(memory_space=pltpu.HBM)],
        out_specs=[pl.BlockSpec(memory_space=pltpu.VMEM)] * len(steps),
        scratch_shapes=[pltpu.SemaphoreType.DMA((len(steps),))],
        compiler_params=pltpu.CompilerParams(vmem_limit_bytes=SMALL_LIMIT),
        name="raw_fields",
    )(pltpu.with_memory_space_constraint(view, pltpu.HBM))


def arrived_kernel(rows, split, step, raw_ref, mix_ref, mask_ref, table_ref, row_ref, out_ref):
    levels = mix_ref.shape[1]
    part = levels // split
    radix = out_ref.shape[3] // LANES
    me = lax.axis_index("lat")
    chip = me // split
    core = lax.rem(me, split)
    starts = [pl.multiple_of(jnp.bitwise_xor(core, c) * part, part) for c in range(split)]
    left = halves(jnp.concatenate([mix_ref[chip, pl.ds(start, part), :] for start in starts], axis=0))
    blocks = [out_ref.at[c] for c in range(split)]
    for r in range(rows):
        mixed = split_product(left, halves(field_rows(raw_ref, 0, levels, r, rows, radix)))
        for c in range(split):
            blocks[c][r] = mixed[c * part : (c + 1) * part]
    source = jnp.bitwise_xor(chip, step_mask(chip, step)) * split + core
    filter_blocks([source * rows + r for r in range(rows)], blocks, mask_ref, table_ref, row_ref)


def arrived_blocks(raw, vertical_mix, polar_mask, tables, lon, rows, split, step):
    vmem = pl.BlockSpec(memory_space=pltpu.VMEM)
    return pl.pallas_call(
        functools.partial(arrived_kernel, rows, split, step),
        out_shape=pltpu.VMEM((split, rows, vertical_mix.shape[1] // split, lon), F32),
        in_specs=[vmem, vmem, pl.BlockSpec(memory_space=pltpu.SMEM), vmem, vmem],
        out_specs=vmem,
        compiler_params=pltpu.CompilerParams(vmem_limit_bytes=VMEM_LIMIT),
        name="arrived_blocks",
    )(raw, vertical_mix, polar_mask, *tables)


def collect_kernel(*refs):
    out_ref = refs[-1]
    for i, ref in enumerate(refs[:-1]):
        out_ref[i] = ref[1] if len(ref.shape) == len(out_ref.shape) else ref[...]


def collect(blocks):
    vmem = pl.BlockSpec(memory_space=pltpu.VMEM)
    return pl.pallas_call(
        collect_kernel,
        out_shape=pltpu.VMEM((len(blocks),) + blocks[0].shape[1:], F32),
        in_specs=[vmem] * len(blocks),
        out_specs=vmem,
        compiler_params=pltpu.CompilerParams(vmem_limit_bytes=SMALL_LIMIT),
        name="collect",
    )(*blocks)


def ocean_kernel(lat_count, split, bounds_ref, own_ref, *refs):
    near_refs, out_ref = refs[:-1], refs[-1]
    rows = own_ref.shape[0]
    slots = out_ref.shape[0]
    half = rows // 2
    me = lax.axis_index("lat")
    start = bounds_ref[me] - half
    length = bounds_ref[me + 1] - bounds_ref[me] + 2 * half + 1
    shift = start - (me - 1) * rows
    first, last = ([ref[r] for r in range(rows)] for ref in near_refs)
    if split > 1:
        upper = lax.rem(me, split) == 0
        first, last = (
            [jnp.where(upper, outer, other) for outer, other in zip(last, first)],
            [jnp.where(upper, other, outer) for outer, other in zip(last, first)],
        )
    near = first + [own_ref[r] for r in range(rows)] + last
    for s in range(slots):
        row = start + s
        valid = (s < length) & (row >= 0) & (row < lat_count)
        picked = jnp.zeros_like(near[0])
        for p, value in enumerate(near):
            picked = jnp.where(valid & (shift + s == p), value, picked)
        out_ref[s] = picked


def neighbour_rows(weighted, device_count, split):
    ends = device_count - 1
    if split == 2:
        pairs = [(i, i + 1) for i in range(1, ends, 2)]
        return [
            lax.ppermute(weighted, "lat", [(i, i ^ 1) for i in range(device_count)]),
            lax.ppermute(weighted, "lat", pairs + [(j, i) for i, j in pairs]),
        ]
    return [
        lax.ppermute(weighted, "lat", [(i, i + 1) for i in range(ends)]),
        lax.ppermute(weighted, "lat", [(i + 1, i) for i in range(ends)]),
    ]


def ocean_slots(weighted, near, band_bounds, lat_count, split):
    rows, flux_count, lon = weighted.shape
    vmem = pl.BlockSpec(memory_space=pltpu.VMEM)
    return pl.pallas_call(
        functools.partial(ocean_kernel, lat_count, split),
        out_shape=jax.ShapeDtypeStruct((3 * rows, flux_count, lon), F32),
        in_specs=[pl.BlockSpec(memory_space=pltpu.SMEM)] + [vmem] * 3,
        out_specs=vmem,
        compiler_params=pltpu.CompilerParams(vmem_limit_bytes=SMALL_LIMIT),
        name="ocean",
    )(band_bounds, weighted, *near)


def place_kernel(split, sources, *refs):
    out_ref, buffer, sems = refs[-3:]
    part, lon = refs[0].shape[-2:]
    rows = refs[0].shape[-3]
    radix = lon // LANES
    chip_rows = rows * split
    tile = radix * SUBLANES
    span = out_ref.shape[0] // part
    me = lax.axis_index("lat")
    chip = me // split
    core = lax.rem(me, split)
    groups = chip_rows * len(sources) // SUBLANES
    chips = len(sources) // groups
    step_groups = [{first // chips, second // chips} for first, second in STEPS] + [{0}]
    pending = {group: sum(group in held for held in step_groups) for group in range(groups)}
    copies = []
    for step in [len(STEPS)] + list(range(len(STEPS))):
        source = jnp.bitwise_xor(chip, step_mask(chip, step))
        base = source // chips * (part * tile) + lax.rem(source, chips) * chip_rows
        for c, (operand, index) in enumerate(sources[step]):
            ref = refs[operand] if index is None else refs[operand].at[index]
            for r in range(rows):
                row = base + jnp.bitwise_xor(core, c) * rows + r
                for t in range(radix):
                    buffer[pl.ds(row + t * SUBLANES, part, stride=tile), :] = ref[
                        r, :, t * LANES : (t + 1) * LANES
                    ]
        for group in step_groups[step]:
            pending[group] -= 1
            if pending[group]:
                continue
            place = jnp.bitwise_xor(chip // chips, group)
            for f in range(part):
                copy = pltpu.make_async_copy(
                    buffer.at[pl.ds(pl.multiple_of((place * part + f) * tile, SUBLANES), tile)],
                    out_ref.at[pl.ds(pl.multiple_of(f * span + place * tile, SUBLANES), tile)],
                    sems.at[group, f],
                )
                copy.start()
                copies.append(copy)
    for copy in copies:
        copy.wait()


def place(operands, sources, lat_count, after):
    part, lon = operands[0].shape[-2:]
    size = part * lat_count * lon // LANES
    groups = lat_count // SUBLANES
    vmem = pl.BlockSpec(memory_space=pltpu.VMEM)
    out = pl.pallas_call(
        functools.partial(place_kernel, len(sources[0]), sources),
        out_shape=jax.ShapeDtypeStruct((size, LANES), F32),
        in_specs=[vmem] * len(operands) + [pl.BlockSpec(memory_space=pl.ANY)],
        out_specs=pl.BlockSpec(memory_space=pltpu.HBM),
        scratch_shapes=[pltpu.VMEM((size, LANES), F32), pltpu.SemaphoreType.DMA((groups, part))],
        compiler_params=pltpu.CompilerParams(vmem_limit_bytes=VMEM_LIMIT),
        name="place",
    )(*operands, pltpu.with_memory_space_constraint(after, pltpu.HBM))
    tiles = out.reshape(part, groups, lon // LANES, SUBLANES, LANES)
    return tiles.transpose(0, 1, 3, 2, 4).reshape(part, lat_count, lon)


def body(device_count, state, vertical_mix, coupling, fractions, weight_index, band_bounds, polar_mask):
    field_count, level_count = vertical_mix.shape[:2]
    stack_count, row_count, lon_count = state.shape
    lat_count = polar_mask.shape[0]
    part = stack_count // device_count
    tables = transform_tables(lon_count, lat_count)
    radix = lon_count // LANES
    blocked = with_layout_constraint(
        state.reshape(stack_count, row_count, radix, LANES), Layout(major_to_minor=(0, 2, 1, 3))
    )
    view = blocked.transpose(0, 2, 1, 3).reshape(-1, LANES)
    mixed = functools.partial(
        mixed_blocks,
        view,
        vertical_mix,
        polar_mask,
        coupling,
        fractions,
        weight_index,
        tables,
        lon_count,
        row_count,
    )

    if part == SUBLANES and level_count == 2 * part and field_count == len(STEPS) + 1:
        split = 2
        raw = raw_fields(view, field_count, split, tuple(range(RAW_STEPS)))
        *blocks, near, far, weighted = mixed(split, RAW_STEPS, len(STEPS) - RAW_STEPS)
        neighbours = neighbour_rows(weighted, device_count, split)
        blocks = list(raw) + blocks
        for step, block in enumerate(blocks):
            if step == HALO_STEP:
                block, *neighbours = lax.optimization_barrier((block, *neighbours))
            if step == RAW_TIE:
                block, *blocks[:RAW_STEPS] = lax.optimization_barrier((block, *blocks[:RAW_STEPS]))
            pairs = [(i, i ^ split * step_mask(i // split, step)) for i in range(device_count)]
            blocks[step] = lax.ppermute(block, "lat", pairs)
        for step in range(RAW_STEPS):
            blocks[step] = arrived_blocks(
                blocks[step], vertical_mix, polar_mask, tables, lon_count, row_count, split, step
            )
        operands = blocks + [near]
        sources = [[(step, 0)] for step in range(len(STEPS))] + [[(len(STEPS), None)]]
        for number, group in enumerate(SWAPS):
            if number == HALO_SWAP:
                last = max(step for step in group if step < len(STEPS))
                blocks[last], *neighbours = lax.optimization_barrier((blocks[last], *neighbours))
            held = collect([(blocks + [far])[step] for step in group])
            for i, step in enumerate(group):
                sources[step].append((len(operands), i))
            operands.append(lax.ppermute(held, "lat", [(i, i ^ 1) for i in range(device_count)]))
        ocean = ocean_slots(weighted, neighbours, band_bounds, lat_count, split)
        state_out = place(operands, sources, lat_count, ocean)
    else:
        *blocks, weighted = mixed(1, 0, field_count)
        stacked = jnp.concatenate(blocks, axis=1)
        moved = lax.all_to_all(stacked, "lat", split_axis=1, concat_axis=0, tiled=True)
        state_out = jnp.transpose(moved, (1, 0, 2))
        neighbours = neighbour_rows(weighted, device_count, 1)
        ocean = ocean_slots(weighted, neighbours, band_bounds, lat_count, 1)
    return (state_out, jnp.transpose(ocean, (1, 0, 2)))


def solution(mesh):
    return jax.shard_map(
        functools.partial(body, mesh.shape["lat"]),
        mesh=mesh,
        in_specs=(P("member", "lat", None), P(), P(), P(), P(("member", "lat")), P(), P()),
        out_specs=(P(("member", "lat"), None, None), P(None, ("member", "lat"), None)),
        check_vma=False,
    )
```

```python
import functools

import jax
import jax.numpy as jnp
import numpy as np
from jax import lax
from jax.experimental import pallas as pl
from jax.experimental.layout import Layout, with_layout_constraint
from jax.experimental.pallas import tpu as pltpu
from jax.sharding import PartitionSpec as P

COSCUT = 0.5
LANES = 128
SUBLANES = 8
STEPS = ((4, 4), (6, 6), (1, 1), (5, 5), (2, 2), (3, 3), (7, 7))
CORE, OUTER, FAR = 8, 9, 10
ORDER = (0, 1, 2, 3, 4, 5, 6, OUTER, CORE, FAR)
WINDOW = 5
F32 = jnp.float32
BF16 = jnp.bfloat16
NORMAL = (((1,), (0,)), ((), ()))
TRANSPOSED = (((1,), (1,)), ((), ()))
VMEM_LIMIT = 32 << 20
SMALL_LIMIT = 8 << 20


def halves(values):
    high = values.astype(BF16)
    return high, (values - high.astype(F32)).astype(BF16)


def split_product(left, right, dims=NORMAL):
    dot = functools.partial(lax.dot_general, dimension_numbers=dims, preferred_element_type=F32)
    return dot(left[0], right[0]) + (dot(left[0], right[1]) + dot(left[1], right[0]))


def np_halves(values):
    values = np.asarray(values, np.float32)
    high = values.astype(jnp.bfloat16)
    return np.stack([high, (values - high.astype(np.float32)).astype(jnp.bfloat16)])


def transform_tables(lon_count, lat_count):
    radix = lon_count // LANES
    steps = radix // 2
    b = np.arange(LANES)[:, None]
    k2 = np.arange(LANES)[None, :]
    table = np.zeros((steps * 2 * LANES + LANES, 2 * LANES))
    for k in range(1, steps + 1):
        angle = 2 * np.pi * ((b * (k + radix * k2)) % lon_count) / lon_count
        c, s = np.cos(angle), np.sin(angle)
        table[(k - 1) * 2 * LANES : k * 2 * LANES] = np.block([[c, -s], [s, c]])
    half = LANES // 2
    angle = 2 * np.pi * ((b * k2) % LANES) / LANES
    table[steps * 2 * LANES :, :LANES] = np.concatenate(
        [np.cos(angle[:, : half + 1]), np.sin(angle[:, 1:half])], axis=1
    )
    wave = np.zeros((steps + 1, 2 * LANES))
    scale = np.full((steps + 1, 2 * LANES), 2.0 / lon_count)
    wave[0, :LANES] = np.concatenate([np.arange(half + 1), np.arange(1, half)]) * radix
    scale[0, [0, half]] = 1.0 / lon_count
    for k in range(1, steps + 1):
        wave[k] = np.tile(k + radix * np.arange(LANES), 2)
    limit = COSCUT**2 * np.sin(np.pi * wave / lon_count) ** 2
    latitude = np.pi * ((np.arange(lat_count) + 0.5) / lat_count - 0.5)
    square = np.repeat(np.cos(latitude)[:, None] ** 2, 2 * LANES, axis=1)
    rows = np.concatenate([limit, scale, square])
    rows = np.pad(rows, ((0, -len(rows) % SUBLANES), (0, 0)))
    return np_halves(table), rows.astype(np.float32)


def filtered(fields, squares, table_ref, row_ref):
    radix = fields.shape[1] // LANES
    half = radix // 2
    height = fields.shape[0] // len(squares)
    parts = [fields[:, a * LANES : (a + 1) * LANES] for a in range(radix)]
    sums = [parts[a] + parts[radix - a] for a in range(1, half + 1)]
    gaps = [parts[a] - parts[radix - a] for a in range(1, half + 1)]

    def pair(k):
        if k == 0:
            rows, width = slice(half * 2 * LANES, half * 2 * LANES + LANES), LANES
        else:
            rows, width = slice((k - 1) * 2 * LANES, k * 2 * LANES), 2 * LANES
        return table_ref[0, rows, :width], table_ref[1, rows, :width]

    def gain(k, width):
        limit = row_ref[k : k + 1, :LANES]
        scale = row_ref[half + 1 + k : half + 2 + k, :LANES]
        groups = [
            jnp.broadcast_to(square / jnp.maximum(square, limit) * scale, (height, LANES))
            for square in squares
        ]
        groups = jnp.concatenate(groups, axis=0)
        return groups if width == LANES else jnp.concatenate([groups, groups], axis=1)

    total = parts[0]
    for value in sums:
        total = total + value
    spectrum = split_product(halves(total), pair(0)) * gain(0, LANES)
    base = split_product(halves(spectrum), pair(0), TRANSPOSED)
    cosines, sines = [], []
    for k in range(1, half + 1):
        real, imag = parts[0], None
        for a in range(1, half + 1):
            angle = 2 * np.pi * (a * k % radix) / radix
            real = real + float(np.cos(angle)) * sums[a - 1]
            term = float(-np.sin(angle)) * gaps[a - 1]
            imag = term if imag is None else imag + term
        both = jnp.concatenate([real, imag], axis=1)
        spectrum = split_product(halves(both), pair(k)) * gain(k, 2 * LANES)
        series = split_product(halves(spectrum), pair(k), TRANSPOSED)
        cosines.append(series[:, :LANES])
        sines.append(series[:, LANES:])
    whole = base
    for value in cosines:
        whole = whole + value
    lower, upper = [], []
    for a in range(1, half + 1):
        even, odd = base, None
        for k in range(1, half + 1):
            angle = 2 * np.pi * (a * k % radix) / radix
            even = even + float(np.cos(angle)) * cosines[k - 1]
            term = float(np.sin(angle)) * sines[k - 1]
            odd = term if odd is None else odd + term
        lower.append(even - odd)
        upper.append(even + odd)
    return jnp.concatenate([whole] + lower + upper[::-1], axis=1)


def filter_blocks(rows, out_refs, mask_ref, table_ref, row_ref):
    part = out_refs[0].shape[1]
    height = len(out_refs) * part
    radix = out_refs[0].shape[2] // LANES
    first_square = 2 * (radix // 2 + 1)
    active = [mask_ref[row] == 1 for row in rows]

    @pl.when(functools.reduce(jnp.logical_or, active))
    def _():
        fields = jnp.concatenate([ref[r] for r in range(len(rows)) for ref in out_refs], axis=0)
        squares = [row_ref[pl.ds(first_square + row, 1), :][:, :LANES] for row in rows]
        smooth = filtered(fields, squares, table_ref, row_ref)
        for r in range(len(rows)):

            @pl.when(active[r])
            def _():
                for i, ref in enumerate(out_refs):
                    start = r * height + i * part
                    ref[r] = smooth[start : start + part]


def step_mask(chip, step):
    first, second = STEPS[step] if step < len(STEPS) else (0, 0)
    if first == second:
        return first
    if isinstance(chip, int):
        return first if (chip >> 2 ^ chip >> 1) & 1 else second
    return jnp.where(lax.rem(chip // 4 + chip // 2, 2) == 1, first, second)


def field_rows(ref, start, count, r, rows, radix):
    step = rows * radix
    return jnp.concatenate(
        [ref[pl.ds(start * step + t * rows + r, count, stride=step), :] for t in range(radix)], axis=1
    )


def spread(values, groups, width, count):
    lane = lax.broadcasted_iota(jnp.int32, (width, width * count), 1)
    repeat = (lax.rem(lane, width) == lax.broadcasted_iota(jnp.int32, lane.shape, 0)).astype(BF16)
    lane_group = lax.broadcasted_iota(jnp.int32, (1, width * count), 1) // width
    keep = jnp.concatenate(
        [
            jnp.broadcast_to((lane_group == group).astype(F32), (height, width * count))
            for group, height in groups
        ],
        axis=0,
    )
    return [
        (jnp.dot(value, repeat, preferred_element_type=F32) * keep).astype(BF16) for value in halves(values)
    ]


def mix_kernel(rows, split, first, *refs):
    inputs, siblings, refs = refs[:9], refs[9 : 8 + split], refs[8 + split :]
    outs = len(refs) - 12
    out_refs, (flux_ref, pick_ref), refs = refs[:outs], refs[outs : outs + 2], refs[outs + 2 :]
    (load, mix_ref, mask_ref, bounds_ref, coupling_ref, fractions_ref, index_ref) = refs[:7]
    table_ref, row_ref, sems = refs[7:]
    copies = [
        pltpu.make_async_copy(source, target, sems.at[i])
        for i, (source, target) in enumerate(zip(inputs, refs[:-1]))
    ]
    for copy in copies:
        copy.start()
    fields, levels, _ = mix_ref.shape
    part = levels // split
    lon = flux_ref.shape[2]
    radix = lon // LANES
    me = lax.axis_index("lat")
    chip = me // split
    core = lax.rem(me, split)
    chosen, weights = [], []
    copies[1].wait()
    start = pl.multiple_of(core * part, part)
    for step in range(first, fields):
        field = jnp.bitwise_xor(chip, step_mask(chip, step)) if split > 1 else step
        weights.append(mix_ref[field, pl.ds(start, part), :])
        chosen.append((field, part))
    weights += [mix_ref[f, levels - 1 : levels, :] for f in range(fields)]
    chosen += [(f, 1) for f in range(fields)]
    left = spread(jnp.concatenate(weights, axis=0), chosen, levels, fields)
    copies[0].wait()
    bottoms = []
    for i, source in enumerate([load] + list(siblings)):
        for r in range(rows):
            mixed = split_product(left, halves(field_rows(source, 0, fields * levels, r, rows, radix)))
            row = jnp.bitwise_xor(core, i) * rows + r if split > 1 else r
            for j, ref in enumerate(out_refs):
                ref[row] = mixed[j * part : (j + 1) * part]
            if i == 0:
                bottoms.append(mixed[outs * part :])
    for copy in copies[2:]:
        copy.wait()
    for r, bottom in enumerate(bottoms):
        speed = jnp.sqrt(bottom[0:1] * bottom[0:1] + bottom[1:2] * bottom[1:2] + 1.0)
        flux = split_product(halves(coupling_ref[...]), halves(bottom))
        flux_ref[r] = speed * flux * fractions_ref[pl.ds(index_ref[r], 1), :]
    first_row = bounds_ref[me] - rows // 2
    length = bounds_ref[me + 1] - first_row + rows // 2 + 1
    for s in range(3 * rows):
        row = first_row + s
        valid = (s < length) & (row >= 0) & (row < mask_ref.shape[0])
        pick_ref[s] = jnp.full(pick_ref.shape[1:], jnp.where(valid, row - (me - 1) * rows, -1))
    filter_blocks(
        [chip * split * rows + r for r in range(split * rows)], out_refs, mask_ref, table_ref, row_ref
    )


def mixed_blocks(
    view, vertical_mix, polar_mask, band_bounds, coupling, fractions, weight_index, tables, lon, rows, siblings, first
):
    split = 1 + len(siblings)
    fields, levels, _ = vertical_mix.shape
    arrays = (view, vertical_mix, polar_mask, band_bounds, coupling, fractions, weight_index) + tuple(
        jnp.asarray(table) for table in tables
    )
    operands = [pltpu.with_memory_space_constraint(value, pltpu.HBM) for value in arrays]
    spaces = [pltpu.SMEM if value.dtype == jnp.int32 else pltpu.VMEM for value in arrays]
    outs = [pltpu.VMEM((rows * split, levels // split, lon), F32)] * (fields - first)
    outs += [
        pltpu.VMEM((rows, coupling.shape[0], lon), F32),
        pltpu.VMEM((3 * rows, coupling.shape[0], LANES), jnp.int32),
    ]
    return pl.pallas_call(
        functools.partial(mix_kernel, rows, split, first),
        out_shape=outs,
        in_specs=[pl.BlockSpec(memory_space=pltpu.HBM)] * len(operands)
        + [pl.BlockSpec(memory_space=pltpu.VMEM)] * len(siblings),
        out_specs=[pl.BlockSpec(memory_space=pltpu.VMEM)] * len(outs),
        scratch_shapes=[space(value.shape, value.dtype) for space, value in zip(spaces, arrays)]
        + [pltpu.SemaphoreType.DMA((len(arrays),))],
        compiler_params=pltpu.CompilerParams(vmem_limit_bytes=VMEM_LIMIT),
        name="mixed_blocks",
    )(*operands, *siblings)


def pick_kernel(split, steps, view_ref, *refs):
    out_refs, sems = refs[:-1], refs[-1]
    span = out_refs[0].shape[0]
    chip = lax.axis_index("lat") // split
    copies = []
    for i, step in enumerate(steps):
        start = pl.multiple_of(jnp.bitwise_xor(chip, step_mask(chip, step)) * span, span)
        copies.append(pltpu.make_async_copy(view_ref.at[pl.ds(start, span)], out_refs[i], sems.at[i]))
        copies[-1].start()
    for copy in copies:
        copy.wait()


def raw_fields(view, field_count, split, steps):
    shape = (view.shape[0] // field_count, LANES)
    return pl.pallas_call(
        functools.partial(pick_kernel, split, steps),
        out_shape=[pltpu.VMEM(shape, F32)] * len(steps),
        in_specs=[pl.BlockSpec(memory_space=pltpu.HBM)],
        out_specs=[pl.BlockSpec(memory_space=pltpu.VMEM)] * len(steps),
        scratch_shapes=[pltpu.SemaphoreType.DMA((len(steps),))],
        compiler_params=pltpu.CompilerParams(vmem_limit_bytes=SMALL_LIMIT),
        name="raw_fields",
    )(pltpu.with_memory_space_constraint(view, pltpu.HBM))


def arrived_kernel(rows, split, step, raw_ref, mix_ref, mask_ref, table_ref, row_ref, *blocks):
    levels = mix_ref.shape[1]
    part = levels // split
    radix = blocks[0].shape[2] // LANES
    me = lax.axis_index("lat")
    chip = me // split
    core = lax.rem(me, split)
    starts = [pl.multiple_of(jnp.bitwise_xor(core, c) * part, part) for c in range(split)]
    left = halves(jnp.concatenate([mix_ref[chip, pl.ds(start, part), :] for start in starts], axis=0))
    for r in range(rows):
        mixed = split_product(left, halves(field_rows(raw_ref, 0, levels, r, rows, radix)))
        for c in range(split):
            blocks[c][r] = mixed[c * part : (c + 1) * part]
    source = jnp.bitwise_xor(chip, step_mask(chip, step)) * split + core
    filter_blocks([source * rows + r for r in range(rows)], blocks, mask_ref, table_ref, row_ref)


def arrived_blocks(raw, vertical_mix, polar_mask, tables, lon, rows, split, step):
    vmem = pl.BlockSpec(memory_space=pltpu.VMEM)
    return pl.pallas_call(
        functools.partial(arrived_kernel, rows, split, step),
        out_shape=[pltpu.VMEM((rows, vertical_mix.shape[1] // split, lon), F32)] * split,
        in_specs=[vmem, vmem, pl.BlockSpec(memory_space=pltpu.SMEM), vmem, vmem],
        out_specs=[vmem] * split,
        compiler_params=pltpu.CompilerParams(vmem_limit_bytes=VMEM_LIMIT),
        name="arrived_blocks",
    )(raw, vertical_mix, polar_mask, *tables)


def fill_slots(split, pick_ref, own_ref, first_ref, last_ref, out_ref):
    slots, flux_count, lon = out_ref.shape
    rows = own_ref.shape[0]
    upper = lax.rem(lax.axis_index("lat"), split) == 0
    for t in range(lon // LANES):
        lanes = slice(t * LANES, (t + 1) * LANES)
        first, last = ([ref[r, :, lanes] for r in range(rows)] for ref in (first_ref, last_ref))
        if split > 1:
            first, last = (
                [jnp.where(upper, outer, other) for outer, other in zip(last, first)],
                [jnp.where(upper, other, outer) for outer, other in zip(last, first)],
            )
        near = first + [own_ref[r, :, lanes] for r in range(rows)] + last
        for s in range(slots):
            pick = pick_ref[s]
            picked = jnp.zeros((flux_count, LANES), F32)
            for p, value in enumerate(near):
                picked = jnp.where(pick == p, value, picked)
            out_ref[s, :, lanes] = picked


def neighbour_rows(weighted, device_count):
    ends = device_count - 1
    return [
        lax.ppermute(weighted, "lat", [(i, i + 1) for i in range(ends)]),
        lax.ppermute(weighted, "lat", [(i + 1, i) for i in range(ends)]),
    ]


def ocean_slots(picks, weighted, near):
    vmem = pl.BlockSpec(memory_space=pltpu.VMEM)
    return pl.pallas_call(
        functools.partial(fill_slots, 1),
        out_shape=jax.ShapeDtypeStruct(picks.shape[:2] + weighted.shape[2:], F32),
        in_specs=[vmem] * 4,
        out_specs=vmem,
        compiler_params=pltpu.CompilerParams(vmem_limit_bytes=SMALL_LIMIT),
        name="ocean",
    )(picks, weighted, *near)


def place_kernel(split, sources, *refs):
    out_ref, ocean_ref, buffer, slots, sems, slots_sem = refs[-6:]
    surface = refs[-10:-6]
    part, lon = refs[0].shape[1:]
    rows = surface[1].shape[0]
    radix = lon // LANES
    chip_rows = rows * split
    tile = radix * SUBLANES
    span = out_ref.shape[0] // part
    me = lax.axis_index("lat")
    chip = me // split
    core = lax.rem(me, split)
    groups = chip_rows * len(sources) // SUBLANES
    chips = len(sources) // groups
    step_groups = [{first // chips, second // chips} for first, second in STEPS] + [{0}]
    pending = {group: sum(group in held for held in step_groups) for group in range(groups)}
    copies = []
    for step in [len(STEPS)] + list(range(len(STEPS))):
        source = jnp.bitwise_xor(chip, step_mask(chip, step))
        base = source // chips * (part * tile) + lax.rem(source, chips) * chip_rows
        for c, operand in enumerate(sources[step]):
            ref = refs[operand]
            for r in range(ref.shape[0]):
                row = base + (r if len(sources[step]) == 1 else jnp.bitwise_xor(core, c) * rows + r)
                for t in range(radix):
                    buffer[pl.ds(row + t * SUBLANES, part, stride=tile), :] = ref[
                        r, :, t * LANES : (t + 1) * LANES
                    ]
        for group in step_groups[step]:
            pending[group] -= 1
            if pending[group]:
                continue
            place = jnp.bitwise_xor(chip // chips, group)
            for f in range(part):
                copy = pltpu.make_async_copy(
                    buffer.at[pl.ds(pl.multiple_of((place * part + f) * tile, SUBLANES), tile)],
                    out_ref.at[pl.ds(pl.multiple_of(f * span + place * tile, SUBLANES), tile)],
                    sems.at[group, f],
                )
                copy.start()
                copies.append(copy)
    fill_slots(split, *surface, slots)
    copies.append(pltpu.make_async_copy(slots, ocean_ref, slots_sem))
    copies[-1].start()
    for copy in copies:
        copy.wait()


def place(operands, sources, lat_count, surface):
    part, lon = operands[0].shape[1:]
    size = part * lat_count * lon // LANES
    groups = lat_count // SUBLANES
    vmem = pl.BlockSpec(memory_space=pltpu.VMEM)
    slots = surface[0].shape[:2] + (lon,)
    out, ocean = pl.pallas_call(
        functools.partial(place_kernel, 2, sources),
        out_shape=[jax.ShapeDtypeStruct((size, LANES), F32), jax.ShapeDtypeStruct(slots, F32)],
        in_specs=[vmem] * (len(operands) + len(surface)),
        out_specs=[pl.BlockSpec(memory_space=pltpu.HBM)] * 2,
        scratch_shapes=[
            pltpu.VMEM((size, LANES), F32),
            pltpu.VMEM(slots, F32),
            pltpu.SemaphoreType.DMA((groups, part)),
            pltpu.SemaphoreType.DMA,
        ],
        compiler_params=pltpu.CompilerParams(vmem_limit_bytes=VMEM_LIMIT),
        name="place",
    )(*operands, *surface)
    tiles = out.reshape(part, groups, lon // LANES, SUBLANES, LANES)
    return tiles.transpose(0, 1, 3, 2, 4).reshape(part, lat_count, lon), ocean


def body(device_count, state, vertical_mix, coupling, fractions, weight_index, band_bounds, polar_mask):
    field_count, level_count = vertical_mix.shape[:2]
    stack_count, row_count, lon_count = state.shape
    lat_count = polar_mask.shape[0]
    part = stack_count // device_count
    tables = transform_tables(lon_count, lat_count)
    radix = lon_count // LANES
    blocked = with_layout_constraint(
        state.reshape(stack_count, row_count, radix, LANES), Layout(major_to_minor=(0, 2, 1, 3))
    )
    view = blocked.transpose(0, 2, 1, 3).reshape(-1, LANES)
    mixed = functools.partial(
        mixed_blocks,
        view,
        vertical_mix,
        polar_mask,
        band_bounds,
        coupling,
        fractions,
        weight_index,
        tables,
        lon_count,
        row_count,
    )

    if part == SUBLANES and level_count == 2 * part and field_count == len(STEPS) + 1:
        split = 2
        swap = [(i, i ^ 1) for i in range(device_count)]
        sibling = lax.ppermute(view, "lat", swap)
        raw = raw_fields(view, field_count, split, (0,))
        *blocks, weighted, picks = mixed((sibling,), 1)
        blocks = dict(enumerate(list(raw) + blocks))
        pairs = [(i, i + 1) for i in range(1, device_count - 1, 2)]
        pairs = {CORE: swap, OUTER: pairs + [(j, i) for i, j in pairs], FAR: swap}
        blocks |= {CORE: weighted, OUTER: weighted}
        for step in range(len(STEPS)):
            pairs[step] = [(i, i ^ split * step_mask(i // split, step)) for i in range(device_count)]
        for place_in_order, item in enumerate(ORDER):
            if item == FAR:
                blocks[0], blocks[FAR] = arrived_blocks(
                    blocks[0], vertical_mix, polar_mask, tables, lon_count, row_count, split, 0
                )
            if place_in_order >= WINDOW:
                earlier = ORDER[place_in_order - WINDOW]
                blocks[item], blocks[earlier] = lax.optimization_barrier((blocks[item], blocks[earlier]))
            blocks[item] = lax.ppermute(blocks[item], "lat", pairs[item])
        operands = [blocks[step] for step in range(len(STEPS) + 1)] + [blocks[FAR]]
        sources = [[0, len(STEPS) + 1]] + [[step] for step in range(1, len(STEPS) + 1)]
        surface = (picks, weighted, blocks[CORE], blocks[OUTER])
        state_out, ocean = place(operands, sources, lat_count, surface)
    else:
        *blocks, weighted, picks = mixed((), 0)
        stacked = jnp.concatenate(blocks, axis=1)
        moved = lax.all_to_all(stacked, "lat", split_axis=1, concat_axis=0, tiled=True)
        state_out = jnp.transpose(moved, (1, 0, 2))
        neighbours = neighbour_rows(weighted, device_count)
        ocean = ocean_slots(picks, weighted, neighbours)
    return (state_out, jnp.transpose(ocean, (1, 0, 2)))


def solution(mesh):
    return jax.shard_map(
        functools.partial(body, mesh.shape["lat"]),
        mesh=mesh,
        in_specs=(P("member", "lat", None), P(), P(), P(), P(("member", "lat")), P(), P()),
        out_specs=(P(("member", "lat"), None, None), P(None, ("member", "lat"), None)),
        check_vma=False,
    )
```

```python
import functools

import jax
import jax.numpy as jnp
import numpy as np
from jax import lax
from jax.experimental import pallas as pl
from jax.experimental.layout import Layout, with_layout_constraint
from jax.experimental.pallas import tpu as pltpu
from jax.sharding import PartitionSpec as P

COSCUT = 0.5
LANES = 128
SUBLANES = 8
STEPS = (6, 4, 3, 5, 1, 2, 7)
CORE, OUTER, FAR = 8, 9, 10
ORDER = (0, 1, 2, 3, 4, 5, 6, OUTER, CORE, FAR)
WINDOW = 5
F32 = jnp.float32
BF16 = jnp.bfloat16
NORMAL = (((1,), (0,)), ((), ()))
TRANSPOSED = (((1,), (1,)), ((), ()))
VMEM_LIMIT = 32 << 20
SMALL_LIMIT = 8 << 20


def halves(values):
    high = values.astype(BF16)
    return high, (values - high.astype(F32)).astype(BF16)


def split_product(left, right, dims=NORMAL):
    dot = functools.partial(lax.dot_general, dimension_numbers=dims, preferred_element_type=F32)
    return dot(left[0], right[0]) + (dot(left[0], right[1]) + dot(left[1], right[0]))


def np_halves(values):
    values = np.asarray(values, np.float32)
    high = values.astype(jnp.bfloat16)
    return np.stack([high, (values - high.astype(np.float32)).astype(jnp.bfloat16)])


def transform_tables(lon_count, lat_count):
    radix = lon_count // LANES
    steps = radix // 2
    b = np.arange(LANES)[:, None]
    k2 = np.arange(LANES)[None, :]
    table = np.zeros((steps * 2 * LANES + LANES, 2 * LANES))
    for k in range(1, steps + 1):
        angle = 2 * np.pi * ((b * (k + radix * k2)) % lon_count) / lon_count
        c, s = np.cos(angle), np.sin(angle)
        table[(k - 1) * 2 * LANES : k * 2 * LANES] = np.block([[c, -s], [s, c]])
    half = LANES // 2
    angle = 2 * np.pi * ((b * k2) % LANES) / LANES
    table[steps * 2 * LANES :, :LANES] = np.concatenate(
        [np.cos(angle[:, : half + 1]), np.sin(angle[:, 1:half])], axis=1
    )
    wave = np.zeros((steps + 1, 2 * LANES))
    scale = np.full((steps + 1, 2 * LANES), 2.0 / lon_count)
    wave[0, :LANES] = np.concatenate([np.arange(half + 1), np.arange(1, half)]) * radix
    scale[0, [0, half]] = 1.0 / lon_count
    for k in range(1, steps + 1):
        wave[k] = np.tile(k + radix * np.arange(LANES), 2)
    limit = COSCUT**2 * np.sin(np.pi * wave / lon_count) ** 2
    latitude = np.pi * ((np.arange(lat_count) + 0.5) / lat_count - 0.5)
    square = np.repeat(np.cos(latitude)[:, None] ** 2, 2 * LANES, axis=1)
    rows = np.concatenate([limit, scale, square])
    rows = np.pad(rows, ((0, -len(rows) % SUBLANES), (0, 0)))
    return np_halves(table), rows.astype(np.float32)


def filtered(fields, squares, table_ref, row_ref):
    radix = fields.shape[1] // LANES
    half = radix // 2
    height = fields.shape[0] // len(squares)
    parts = [fields[:, a * LANES : (a + 1) * LANES] for a in range(radix)]
    sums = [parts[a] + parts[radix - a] for a in range(1, half + 1)]
    gaps = [parts[a] - parts[radix - a] for a in range(1, half + 1)]

    def pair(k):
        if k == 0:
            rows, width = slice(half * 2 * LANES, half * 2 * LANES + LANES), LANES
        else:
            rows, width = slice((k - 1) * 2 * LANES, k * 2 * LANES), 2 * LANES
        return table_ref[0, rows, :width], table_ref[1, rows, :width]

    def gain(k, width):
        limit = row_ref[k : k + 1, :LANES]
        scale = row_ref[half + 1 + k : half + 2 + k, :LANES]
        groups = [
            jnp.broadcast_to(square / jnp.maximum(square, limit) * scale, (height, LANES))
            for square in squares
        ]
        groups = jnp.concatenate(groups, axis=0)
        return groups if width == LANES else jnp.concatenate([groups, groups], axis=1)

    total = parts[0]
    for value in sums:
        total = total + value
    spectrum = split_product(halves(total), pair(0)) * gain(0, LANES)
    base = split_product(halves(spectrum), pair(0), TRANSPOSED)
    cosines, sines = [], []
    for k in range(1, half + 1):
        real, imag = parts[0], None
        for a in range(1, half + 1):
            angle = 2 * np.pi * (a * k % radix) / radix
            real = real + float(np.cos(angle)) * sums[a - 1]
            term = float(-np.sin(angle)) * gaps[a - 1]
            imag = term if imag is None else imag + term
        both = jnp.concatenate([real, imag], axis=1)
        spectrum = split_product(halves(both), pair(k)) * gain(k, 2 * LANES)
        series = split_product(halves(spectrum), pair(k), TRANSPOSED)
        cosines.append(series[:, :LANES])
        sines.append(series[:, LANES:])
    whole = base
    for value in cosines:
        whole = whole + value
    lower, upper = [], []
    for a in range(1, half + 1):
        even, odd = base, None
        for k in range(1, half + 1):
            angle = 2 * np.pi * (a * k % radix) / radix
            even = even + float(np.cos(angle)) * cosines[k - 1]
            term = float(np.sin(angle)) * sines[k - 1]
            odd = term if odd is None else odd + term
        lower.append(even - odd)
        upper.append(even + odd)
    return jnp.concatenate([whole] + lower + upper[::-1], axis=1)


def filter_blocks(rows, out_refs, mask_ref, table_ref, row_ref):
    part = out_refs[0].shape[1]
    height = len(out_refs) * part
    radix = out_refs[0].shape[2] // LANES
    first_square = 2 * (radix // 2 + 1)
    active = [mask_ref[row] == 1 for row in rows]

    @pl.when(functools.reduce(jnp.logical_or, active))
    def _():
        fields = jnp.concatenate([ref[r] for r in range(len(rows)) for ref in out_refs], axis=0)
        squares = [row_ref[pl.ds(first_square + row, 1), :][:, :LANES] for row in rows]
        smooth = filtered(fields, squares, table_ref, row_ref)
        for r in range(len(rows)):

            @pl.when(active[r])
            def _():
                for i, ref in enumerate(out_refs):
                    start = r * height + i * part
                    ref[r] = smooth[start : start + part]


def partner(chip, step):
    return chip ^ STEPS[step] if step < len(STEPS) else chip


def field_rows(ref, start, count, r, rows, radix):
    step = rows * radix
    return jnp.concatenate(
        [ref[pl.ds(start * step + t * rows + r, count, stride=step), :] for t in range(radix)], axis=1
    )


def spread(values, groups, width, count):
    lane = lax.broadcasted_iota(jnp.int32, (width, width * count), 1)
    repeat = (lax.rem(lane, width) == lax.broadcasted_iota(jnp.int32, lane.shape, 0)).astype(BF16)
    lane_group = lax.broadcasted_iota(jnp.int32, (1, width * count), 1) // width
    keep = jnp.concatenate(
        [
            jnp.broadcast_to((lane_group == group).astype(F32), (height, width * count))
            for group, height in groups
        ],
        axis=0,
    )
    return [
        (jnp.dot(value, repeat, preferred_element_type=F32) * keep).astype(BF16) for value in halves(values)
    ]


def mix_kernel(rows, split, first, *refs):
    inputs, siblings, refs = refs[:9], refs[9 : 8 + split], refs[8 + split :]
    outs = len(refs) - 12
    out_refs, (flux_ref, pick_ref), refs = refs[:outs], refs[outs : outs + 2], refs[outs + 2 :]
    (load, mix_ref, mask_ref, bounds_ref, coupling_ref, fractions_ref, index_ref) = refs[:7]
    table_ref, row_ref, sems = refs[7:]
    copies = [
        pltpu.make_async_copy(source, target, sems.at[i])
        for i, (source, target) in enumerate(zip(inputs, refs[:-1]))
    ]
    for copy in copies:
        copy.start()
    fields, levels, _ = mix_ref.shape
    part = levels // split
    lon = flux_ref.shape[2]
    radix = lon // LANES
    me = lax.axis_index("lat")
    chip = me // split
    core = lax.rem(me, split)
    chosen, weights = [], []
    copies[1].wait()
    start = pl.multiple_of(core * part, part)
    for step in range(first, fields):
        field = partner(chip, step) if split > 1 else step
        weights.append(mix_ref[field, pl.ds(start, part), :])
        chosen.append((field, part))
    weights += [mix_ref[f, levels - 1 : levels, :] for f in range(fields)]
    chosen += [(f, 1) for f in range(fields)]
    left = spread(jnp.concatenate(weights, axis=0), chosen, levels, fields)
    copies[0].wait()
    bottoms = []
    for i, source in enumerate([load] + list(siblings)):
        for r in range(rows):
            mixed = split_product(left, halves(field_rows(source, 0, fields * levels, r, rows, radix)))
            row = jnp.bitwise_xor(core, i) * rows + r if split > 1 else r
            for j, ref in enumerate(out_refs):
                ref[row] = mixed[j * part : (j + 1) * part]
            if i == 0:
                bottoms.append(mixed[outs * part :])
    for copy in copies[2:]:
        copy.wait()
    for r, bottom in enumerate(bottoms):
        speed = jnp.sqrt(bottom[0:1] * bottom[0:1] + bottom[1:2] * bottom[1:2] + 1.0)
        flux = split_product(halves(coupling_ref[...]), halves(bottom))
        flux_ref[r] = speed * flux * fractions_ref[pl.ds(index_ref[r], 1), :]
    first_row = bounds_ref[me] - rows // 2
    length = bounds_ref[me + 1] - first_row + rows // 2 + 1
    for s in range(3 * rows):
        row = first_row + s
        valid = (s < length) & (row >= 0) & (row < mask_ref.shape[0])
        pick_ref[s] = jnp.full(pick_ref.shape[1:], jnp.where(valid, row - (me - 1) * rows, -1))
    filter_blocks(
        [chip * split * rows + r for r in range(split * rows)], out_refs, mask_ref, table_ref, row_ref
    )


def mixed_blocks(
    view, vertical_mix, polar_mask, band_bounds, coupling, fractions, weight_index, tables, lon, rows, siblings, first
):
    split = 1 + len(siblings)
    fields, levels, _ = vertical_mix.shape
    arrays = (view, vertical_mix, polar_mask, band_bounds, coupling, fractions, weight_index) + tuple(
        jnp.asarray(table) for table in tables
    )
    operands = [pltpu.with_memory_space_constraint(value, pltpu.HBM) for value in arrays]
    spaces = [pltpu.SMEM if value.dtype == jnp.int32 else pltpu.VMEM for value in arrays]
    outs = [pltpu.VMEM((rows * split, levels // split, lon), F32)] * (fields - first)
    outs += [
        pltpu.VMEM((rows, coupling.shape[0], lon), F32),
        pltpu.VMEM((3 * rows, coupling.shape[0], LANES), jnp.int32),
    ]
    return pl.pallas_call(
        functools.partial(mix_kernel, rows, split, first),
        out_shape=outs,
        in_specs=[pl.BlockSpec(memory_space=pltpu.HBM)] * len(operands)
        + [pl.BlockSpec(memory_space=pltpu.VMEM)] * len(siblings),
        out_specs=[pl.BlockSpec(memory_space=pltpu.VMEM)] * len(outs),
        scratch_shapes=[space(value.shape, value.dtype) for space, value in zip(spaces, arrays)]
        + [pltpu.SemaphoreType.DMA((len(arrays),))],
        compiler_params=pltpu.CompilerParams(vmem_limit_bytes=VMEM_LIMIT),
        name="mixed_blocks",
    )(*operands, *siblings)


def pick_kernel(split, steps, view_ref, *refs):
    out_refs, sems = refs[:-1], refs[-1]
    span = out_refs[0].shape[0]
    chip = lax.axis_index("lat") // split
    copies = []
    for i, step in enumerate(steps):
        start = pl.multiple_of(partner(chip, step) * span, span)
        copies.append(pltpu.make_async_copy(view_ref.at[pl.ds(start, span)], out_refs[i], sems.at[i]))
        copies[-1].start()
    for copy in copies:
        copy.wait()


def raw_fields(view, field_count, split, steps):
    shape = (view.shape[0] // field_count, LANES)
    return pl.pallas_call(
        functools.partial(pick_kernel, split, steps),
        out_shape=[pltpu.VMEM(shape, F32)] * len(steps),
        in_specs=[pl.BlockSpec(memory_space=pltpu.HBM)],
        out_specs=[pl.BlockSpec(memory_space=pltpu.VMEM)] * len(steps),
        scratch_shapes=[pltpu.SemaphoreType.DMA((len(steps),))],
        compiler_params=pltpu.CompilerParams(vmem_limit_bytes=SMALL_LIMIT),
        name="raw_fields",
    )(pltpu.with_memory_space_constraint(view, pltpu.HBM))


def arrived_kernel(rows, split, step, raw_ref, mix_ref, mask_ref, table_ref, row_ref, *blocks):
    levels = mix_ref.shape[1]
    part = levels // split
    radix = blocks[0].shape[2] // LANES
    me = lax.axis_index("lat")
    chip = me // split
    core = lax.rem(me, split)
    starts = [pl.multiple_of(jnp.bitwise_xor(core, c) * part, part) for c in range(split)]
    left = halves(jnp.concatenate([mix_ref[chip, pl.ds(start, part), :] for start in starts], axis=0))
    for r in range(rows):
        mixed = split_product(left, halves(field_rows(raw_ref, 0, levels, r, rows, radix)))
        for c in range(split):
            blocks[c][r] = mixed[c * part : (c + 1) * part]
    source = partner(chip, step) * split + core
    filter_blocks([source * rows + r for r in range(rows)], blocks, mask_ref, table_ref, row_ref)


def arrived_blocks(raw, vertical_mix, polar_mask, tables, lon, rows, split, step):
    vmem = pl.BlockSpec(memory_space=pltpu.VMEM)
    return pl.pallas_call(
        functools.partial(arrived_kernel, rows, split, step),
        out_shape=[pltpu.VMEM((rows, vertical_mix.shape[1] // split, lon), F32)] * split,
        in_specs=[vmem, vmem, pl.BlockSpec(memory_space=pltpu.SMEM), vmem, vmem],
        out_specs=[vmem] * split,
        compiler_params=pltpu.CompilerParams(vmem_limit_bytes=VMEM_LIMIT),
        name="arrived_blocks",
    )(raw, vertical_mix, polar_mask, *tables)


def fill_slots(split, pick_ref, own_ref, first_ref, last_ref, out_ref):
    slots, flux_count, lon = out_ref.shape
    rows = own_ref.shape[0]
    upper = lax.rem(lax.axis_index("lat"), split) == 0
    for t in range(lon // LANES):
        lanes = slice(t * LANES, (t + 1) * LANES)
        first, last = ([ref[r, :, lanes] for r in range(rows)] for ref in (first_ref, last_ref))
        if split > 1:
            first, last = (
                [jnp.where(upper, outer, other) for outer, other in zip(last, first)],
                [jnp.where(upper, other, outer) for outer, other in zip(last, first)],
            )
        near = first + [own_ref[r, :, lanes] for r in range(rows)] + last
        for s in range(slots):
            pick = pick_ref[s]
            picked = jnp.zeros((flux_count, LANES), F32)
            for p, value in enumerate(near):
                picked = jnp.where(pick == p, value, picked)
            out_ref[s, :, lanes] = picked


def neighbour_rows(weighted, device_count):
    ends = device_count - 1
    return [
        lax.ppermute(weighted, "lat", [(i, i + 1) for i in range(ends)]),
        lax.ppermute(weighted, "lat", [(i + 1, i) for i in range(ends)]),
    ]


def ocean_slots(picks, weighted, near):
    vmem = pl.BlockSpec(memory_space=pltpu.VMEM)
    return pl.pallas_call(
        functools.partial(fill_slots, 1),
        out_shape=jax.ShapeDtypeStruct(picks.shape[:2] + weighted.shape[2:], F32),
        in_specs=[vmem] * 4,
        out_specs=vmem,
        compiler_params=pltpu.CompilerParams(vmem_limit_bytes=SMALL_LIMIT),
        name="ocean",
    )(picks, weighted, *near)


def place_kernel(split, sources, *refs):
    out_ref, ocean_ref, buffer, slots, sems, slots_sem = refs[-6:]
    surface = refs[-10:-6]
    part, lon = refs[0].shape[1:]
    rows = surface[1].shape[0]
    radix = lon // LANES
    chip_rows = rows * split
    tile = radix * SUBLANES
    me = lax.axis_index("lat")
    chip = me // split
    core = lax.rem(me, split)
    groups = chip_rows * len(sources) // SUBLANES
    chips = len(sources) // groups
    step_groups = [mask // chips for mask in STEPS] + [0]
    pending = [step_groups.count(group) for group in range(groups)]
    copies = []
    for step in [len(STEPS)] + list(range(len(STEPS))):
        source = partner(chip, step)
        base = source // chips * (part * tile) + lax.rem(source, chips) * chip_rows
        for c, operand in enumerate(sources[step]):
            ref = refs[operand]
            for r in range(ref.shape[0]):
                row = base + (r if len(sources[step]) == 1 else jnp.bitwise_xor(core, c) * rows + r)
                for t in range(radix):
                    buffer[pl.ds(row + t * SUBLANES, part, stride=tile), :] = ref[
                        r, :, t * LANES : (t + 1) * LANES
                    ]
        group = step_groups[step]
        pending[group] -= 1
        if not pending[group]:
            place = jnp.bitwise_xor(chip // chips, group)
            copy = pltpu.make_async_copy(
                buffer.at[pl.ds(pl.multiple_of(place * part * tile, SUBLANES), part * tile)].reshape(
                    part, tile, LANES
                ),
                out_ref.at[:, pl.ds(pl.multiple_of(place * tile, SUBLANES), tile)],
                sems.at[group],
            )
            copy.start()
            copies.append(copy)
    fill_slots(split, *surface, slots)
    copies.append(pltpu.make_async_copy(slots, ocean_ref, slots_sem))
    copies[-1].start()
    for copy in copies:
        copy.wait()


def place(operands, sources, lat_count, surface):
    part, lon = operands[0].shape[1:]
    size = part * lat_count * lon // LANES
    groups = lat_count // SUBLANES
    vmem = pl.BlockSpec(memory_space=pltpu.VMEM)
    slots = surface[0].shape[:2] + (lon,)
    out, ocean = pl.pallas_call(
        functools.partial(place_kernel, 2, sources),
        out_shape=[
            jax.ShapeDtypeStruct((part, size // part, LANES), F32),
            jax.ShapeDtypeStruct(slots, F32),
        ],
        in_specs=[vmem] * (len(operands) + len(surface)),
        out_specs=[pl.BlockSpec(memory_space=pltpu.HBM)] * 2,
        scratch_shapes=[
            pltpu.VMEM((size, LANES), F32),
            pltpu.VMEM(slots, F32),
            pltpu.SemaphoreType.DMA((groups,)),
            pltpu.SemaphoreType.DMA,
        ],
        compiler_params=pltpu.CompilerParams(vmem_limit_bytes=VMEM_LIMIT),
        name="place",
    )(*operands, *surface)
    tiles = out.reshape(part, groups, lon // LANES, SUBLANES, LANES)
    return tiles.transpose(0, 1, 3, 2, 4).reshape(part, lat_count, lon), ocean


def body(device_count, state, vertical_mix, coupling, fractions, weight_index, band_bounds, polar_mask):
    field_count, level_count = vertical_mix.shape[:2]
    stack_count, row_count, lon_count = state.shape
    lat_count = polar_mask.shape[0]
    part = stack_count // device_count
    tables = transform_tables(lon_count, lat_count)
    radix = lon_count // LANES
    blocked = with_layout_constraint(
        state.reshape(stack_count, row_count, radix, LANES), Layout(major_to_minor=(0, 2, 1, 3))
    )
    view = blocked.transpose(0, 2, 1, 3).reshape(-1, LANES)
    mixed = functools.partial(
        mixed_blocks,
        view,
        vertical_mix,
        polar_mask,
        band_bounds,
        coupling,
        fractions,
        weight_index,
        tables,
        lon_count,
        row_count,
    )

    if part == SUBLANES and level_count == 2 * part and field_count == len(STEPS) + 1:
        split = 2
        swap = [(i, i ^ 1) for i in range(device_count)]
        sibling = lax.ppermute(view, "lat", swap)
        raw = raw_fields(view, field_count, split, (0,))
        *blocks, weighted, picks = mixed((sibling,), 1)
        blocks = dict(enumerate(list(raw) + blocks))
        pairs = [(i, i + 1) for i in range(1, device_count - 1, 2)]
        pairs = {CORE: swap, OUTER: pairs + [(j, i) for i, j in pairs], FAR: swap}
        blocks |= {CORE: weighted, OUTER: weighted}
        for step in range(len(STEPS)):
            pairs[step] = [(i, split * partner(i // split, step) + i % split) for i in range(device_count)]
        for place_in_order, item in enumerate(ORDER):
            if item == FAR:
                blocks[0], blocks[FAR] = arrived_blocks(
                    blocks[0], vertical_mix, polar_mask, tables, lon_count, row_count, split, 0
                )
            if place_in_order >= WINDOW:
                earlier = ORDER[place_in_order - WINDOW]
                blocks[item], blocks[earlier] = lax.optimization_barrier((blocks[item], blocks[earlier]))
            blocks[item] = lax.ppermute(blocks[item], "lat", pairs[item])
        operands = [blocks[step] for step in range(len(STEPS) + 1)] + [blocks[FAR]]
        sources = [[0, len(STEPS) + 1]] + [[step] for step in range(1, len(STEPS) + 1)]
        surface = (picks, weighted, blocks[CORE], blocks[OUTER])
        state_out, ocean = place(operands, sources, lat_count, surface)
    else:
        *blocks, weighted, picks = mixed((), 0)
        stacked = jnp.concatenate(blocks, axis=1)
        moved = lax.all_to_all(stacked, "lat", split_axis=1, concat_axis=0, tiled=True)
        state_out = jnp.transpose(moved, (1, 0, 2))
        neighbours = neighbour_rows(weighted, device_count)
        ocean = ocean_slots(picks, weighted, neighbours)
    return (state_out, jnp.transpose(ocean, (1, 0, 2)))


def solution(mesh):
    return jax.shard_map(
        functools.partial(body, mesh.shape["lat"]),
        mesh=mesh,
        in_specs=(P("member", "lat", None), P(), P(), P(), P(("member", "lat")), P(), P()),
        out_specs=(P(("member", "lat"), None, None), P(None, ("member", "lat"), None)),
        check_vma=False,
    )
```

```python
import functools

import jax
import jax.numpy as jnp
import numpy as np
from jax import lax
from jax.experimental import pallas as pl
from jax.experimental.layout import Layout, with_layout_constraint
from jax.experimental.pallas import tpu as pltpu
from jax.sharding import PartitionSpec as P

COSCUT = 0.5
LANES = 128
SUBLANES = 8
STEPS = (6, 7, 2, 5, 1, 3, 4)
CORE, OUTER, FAR = 8, 9, 10
ORDER = (0, 1, 2, 3, 4, 5, 6, OUTER, CORE, FAR)
WINDOW = 5
F32 = jnp.float32
BF16 = jnp.bfloat16
NORMAL = (((1,), (0,)), ((), ()))
TRANSPOSED = (((1,), (1,)), ((), ()))
VMEM_LIMIT = 32 << 20
SMALL_LIMIT = 8 << 20


def halves(values):
    high = values.astype(BF16)
    return high, (values - high.astype(F32)).astype(BF16)


def split_product(left, right, dims=NORMAL):
    dot = functools.partial(lax.dot_general, dimension_numbers=dims, preferred_element_type=F32)
    return dot(left[0], right[0]) + (dot(left[0], right[1]) + dot(left[1], right[0]))


def np_halves(values):
    values = np.asarray(values, np.float32)
    high = values.astype(jnp.bfloat16)
    return np.stack([high, (values - high.astype(np.float32)).astype(jnp.bfloat16)])


def transform_tables(lon_count, lat_count):
    radix = lon_count // LANES
    steps = radix // 2
    b = np.arange(LANES)[:, None]
    k2 = np.arange(LANES)[None, :]
    table = np.zeros((steps * 2 * LANES + LANES, 2 * LANES))
    for k in range(1, steps + 1):
        angle = 2 * np.pi * ((b * (k + radix * k2)) % lon_count) / lon_count
        c, s = np.cos(angle), np.sin(angle)
        table[(k - 1) * 2 * LANES : k * 2 * LANES] = np.block([[c, -s], [s, c]])
    half = LANES // 2
    angle = 2 * np.pi * ((b * k2) % LANES) / LANES
    table[steps * 2 * LANES :, :LANES] = np.concatenate(
        [np.cos(angle[:, : half + 1]), np.sin(angle[:, 1:half])], axis=1
    )
    wave = np.zeros((steps + 1, 2 * LANES))
    scale = np.full((steps + 1, 2 * LANES), 2.0 / lon_count)
    wave[0, :LANES] = np.concatenate([np.arange(half + 1), np.arange(1, half)]) * radix
    scale[0, [0, half]] = 1.0 / lon_count
    for k in range(1, steps + 1):
        wave[k] = np.tile(k + radix * np.arange(LANES), 2)
    limit = COSCUT**2 * np.sin(np.pi * wave / lon_count) ** 2
    latitude = np.pi * ((np.arange(lat_count) + 0.5) / lat_count - 0.5)
    square = np.repeat(np.cos(latitude)[:, None] ** 2, 2 * LANES, axis=1)
    rows = np.concatenate([limit, scale, square])
    rows = np.pad(rows, ((0, -len(rows) % SUBLANES), (0, 0)))
    return np_halves(table), rows.astype(np.float32)


def filtered(fields, squares, table_ref, row_ref):
    radix = fields.shape[1] // LANES
    half = radix // 2
    height = fields.shape[0] // len(squares)
    parts = [fields[:, a * LANES : (a + 1) * LANES] for a in range(radix)]
    sums = [parts[a] + parts[radix - a] for a in range(1, half + 1)]
    gaps = [parts[a] - parts[radix - a] for a in range(1, half + 1)]

    def pair(k):
        if k == 0:
            rows, width = slice(half * 2 * LANES, half * 2 * LANES + LANES), LANES
        else:
            rows, width = slice((k - 1) * 2 * LANES, k * 2 * LANES), 2 * LANES
        return table_ref[0, rows, :width], table_ref[1, rows, :width]

    def gain(k, width):
        limit = row_ref[k : k + 1, :LANES]
        scale = row_ref[half + 1 + k : half + 2 + k, :LANES]
        groups = [
            jnp.broadcast_to(square / jnp.maximum(square, limit) * scale, (height, LANES))
            for square in squares
        ]
        groups = jnp.concatenate(groups, axis=0)
        return groups if width == LANES else jnp.concatenate([groups, groups], axis=1)

    total = parts[0]
    for value in sums:
        total = total + value
    spectrum = split_product(halves(total), pair(0)) * gain(0, LANES)
    base = split_product(halves(spectrum), pair(0), TRANSPOSED)
    cosines, sines = [], []
    for k in range(1, half + 1):
        real, imag = parts[0], None
        for a in range(1, half + 1):
            angle = 2 * np.pi * (a * k % radix) / radix
            real = real + float(np.cos(angle)) * sums[a - 1]
            term = float(-np.sin(angle)) * gaps[a - 1]
            imag = term if imag is None else imag + term
        both = jnp.concatenate([real, imag], axis=1)
        spectrum = split_product(halves(both), pair(k)) * gain(k, 2 * LANES)
        series = split_product(halves(spectrum), pair(k), TRANSPOSED)
        cosines.append(series[:, :LANES])
        sines.append(series[:, LANES:])
    whole = base
    for value in cosines:
        whole = whole + value
    lower, upper = [], []
    for a in range(1, half + 1):
        even, odd = base, None
        for k in range(1, half + 1):
            angle = 2 * np.pi * (a * k % radix) / radix
            even = even + float(np.cos(angle)) * cosines[k - 1]
            term = float(np.sin(angle)) * sines[k - 1]
            odd = term if odd is None else odd + term
        lower.append(even - odd)
        upper.append(even + odd)
    return jnp.concatenate([whole] + lower + upper[::-1], axis=1)


def filter_blocks(rows, out_refs, mask_ref, table_ref, row_ref):
    part = out_refs[0].shape[1]
    height = len(out_refs) * part
    radix = out_refs[0].shape[2] // LANES
    first_square = 2 * (radix // 2 + 1)
    active = [mask_ref[row] == 1 for row in rows]

    @pl.when(functools.reduce(jnp.logical_or, active))
    def _():
        fields = jnp.concatenate([ref[r] for r in range(len(rows)) for ref in out_refs], axis=0)
        squares = [row_ref[pl.ds(first_square + row, 1), :][:, :LANES] for row in rows]
        smooth = filtered(fields, squares, table_ref, row_ref)
        for r in range(len(rows)):

            @pl.when(active[r])
            def _():
                for i, ref in enumerate(out_refs):
                    start = r * height + i * part
                    ref[r] = smooth[start : start + part]


def partner(chip, step):
    return chip ^ STEPS[step] if step < len(STEPS) else chip


def field_rows(ref, start, count, r, rows, radix):
    step = rows * radix
    return jnp.concatenate(
        [ref[pl.ds(start * step + t * rows + r, count, stride=step), :] for t in range(radix)], axis=1
    )


def spread(values, groups, width, count):
    lane = lax.broadcasted_iota(jnp.int32, (width, width * count), 1)
    repeat = (lax.rem(lane, width) == lax.broadcasted_iota(jnp.int32, lane.shape, 0)).astype(BF16)
    lane_group = lax.broadcasted_iota(jnp.int32, (1, width * count), 1) // width
    keep = jnp.concatenate(
        [
            jnp.broadcast_to((lane_group == group).astype(F32), (height, width * count))
            for group, height in groups
        ],
        axis=0,
    )
    return [
        (jnp.dot(value, repeat, preferred_element_type=F32) * keep).astype(BF16) for value in halves(values)
    ]


def mix_kernel(rows, split, first, *refs):
    inputs, siblings, refs = refs[:9], refs[9 : 8 + split], refs[8 + split :]
    outs = len(refs) - 12
    out_refs, (flux_ref, pick_ref), refs = refs[:outs], refs[outs : outs + 2], refs[outs + 2 :]
    (load, mix_ref, mask_ref, bounds_ref, coupling_ref, fractions_ref, index_ref) = refs[:7]
    table_ref, row_ref, sems = refs[7:]
    copies = [
        pltpu.make_async_copy(source, target, sems.at[i])
        for i, (source, target) in enumerate(zip(inputs, refs[:-1]))
    ]
    for copy in copies:
        copy.start()
    fields, levels, _ = mix_ref.shape
    part = levels // split
    lon = flux_ref.shape[2]
    radix = lon // LANES
    me = lax.axis_index("lat")
    chip = me // split
    core = lax.rem(me, split)
    chosen, weights = [], []
    copies[1].wait()
    start = pl.multiple_of(core * part, part)
    for step in range(first, fields):
        field = partner(chip, step) if split > 1 else step
        weights.append(mix_ref[field, pl.ds(start, part), :])
        chosen.append((field, part))
    weights += [mix_ref[f, levels - 1 : levels, :] for f in range(fields)]
    chosen += [(f, 1) for f in range(fields)]
    left = spread(jnp.concatenate(weights, axis=0), chosen, levels, fields)
    copies[0].wait()
    bottoms = []
    for i, source in enumerate([load] + list(siblings)):
        for r in range(rows):
            mixed = split_product(left, halves(field_rows(source, 0, fields * levels, r, rows, radix)))
            row = jnp.bitwise_xor(core, i) * rows + r if split > 1 else r
            for j, ref in enumerate(out_refs):
                ref[row] = mixed[j * part : (j + 1) * part]
            if i == 0:
                bottoms.append(mixed[outs * part :])
    for copy in copies[2:]:
        copy.wait()
    for r, bottom in enumerate(bottoms):
        speed = jnp.sqrt(bottom[0:1] * bottom[0:1] + bottom[1:2] * bottom[1:2] + 1.0)
        flux = split_product(halves(coupling_ref[...]), halves(bottom))
        flux_ref[r] = speed * flux * fractions_ref[pl.ds(index_ref[r], 1), :]
    first_row = bounds_ref[me] - rows // 2
    length = bounds_ref[me + 1] - first_row + rows // 2 + 1
    for s in range(3 * rows):
        row = first_row + s
        valid = (s < length) & (row >= 0) & (row < mask_ref.shape[0])
        pick_ref[s] = jnp.full(pick_ref.shape[1:], jnp.where(valid, row - (me - 1) * rows, -1))
    filter_blocks(
        [chip * split * rows + r for r in range(split * rows)], out_refs, mask_ref, table_ref, row_ref
    )


def mixed_blocks(
    view, vertical_mix, polar_mask, band_bounds, coupling, fractions, weight_index, tables, lon, rows, siblings, first
):
    split = 1 + len(siblings)
    fields, levels, _ = vertical_mix.shape
    arrays = (view, vertical_mix, polar_mask, band_bounds, coupling, fractions, weight_index) + tuple(
        jnp.asarray(table) for table in tables
    )
    operands = [pltpu.with_memory_space_constraint(value, pltpu.HBM) for value in arrays]
    spaces = [pltpu.SMEM if value.dtype == jnp.int32 else pltpu.VMEM for value in arrays]
    outs = [pltpu.VMEM((rows * split, levels // split, lon), F32)] * (fields - first)
    outs += [
        pltpu.VMEM((rows, coupling.shape[0], lon), F32),
        pltpu.VMEM((3 * rows, coupling.shape[0], LANES), jnp.int32),
    ]
    return pl.pallas_call(
        functools.partial(mix_kernel, rows, split, first),
        out_shape=outs,
        in_specs=[pl.BlockSpec(memory_space=pltpu.HBM)] * len(operands)
        + [pl.BlockSpec(memory_space=pltpu.VMEM)] * len(siblings),
        out_specs=[pl.BlockSpec(memory_space=pltpu.VMEM)] * len(outs),
        scratch_shapes=[space(value.shape, value.dtype) for space, value in zip(spaces, arrays)]
        + [pltpu.SemaphoreType.DMA((len(arrays),))],
        compiler_params=pltpu.CompilerParams(vmem_limit_bytes=VMEM_LIMIT),
        name="mixed_blocks",
    )(*operands, *siblings)


def pick_kernel(split, steps, view_ref, *refs):
    out_refs, sems = refs[:-1], refs[-1]
    span = out_refs[0].shape[0]
    chip = lax.axis_index("lat") // split
    copies = []
    for i, step in enumerate(steps):
        start = pl.multiple_of(partner(chip, step) * span, span)
        copies.append(pltpu.make_async_copy(view_ref.at[pl.ds(start, span)], out_refs[i], sems.at[i]))
        copies[-1].start()
    for copy in copies:
        copy.wait()


def raw_fields(view, field_count, split, steps):
    shape = (view.shape[0] // field_count, LANES)
    return pl.pallas_call(
        functools.partial(pick_kernel, split, steps),
        out_shape=[pltpu.VMEM(shape, F32)] * len(steps),
        in_specs=[pl.BlockSpec(memory_space=pltpu.HBM)],
        out_specs=[pl.BlockSpec(memory_space=pltpu.VMEM)] * len(steps),
        scratch_shapes=[pltpu.SemaphoreType.DMA((len(steps),))],
        compiler_params=pltpu.CompilerParams(vmem_limit_bytes=SMALL_LIMIT),
        name="raw_fields",
    )(pltpu.with_memory_space_constraint(view, pltpu.HBM))


def arrived_kernel(rows, split, step, raw_ref, mix_ref, mask_ref, table_ref, row_ref, *blocks):
    levels = mix_ref.shape[1]
    part = levels // split
    radix = blocks[0].shape[2] // LANES
    me = lax.axis_index("lat")
    chip = me // split
    core = lax.rem(me, split)
    starts = [pl.multiple_of(jnp.bitwise_xor(core, c) * part, part) for c in range(split)]
    left = halves(jnp.concatenate([mix_ref[chip, pl.ds(start, part), :] for start in starts], axis=0))
    for r in range(rows):
        mixed = split_product(left, halves(field_rows(raw_ref, 0, levels, r, rows, radix)))
        for c in range(split):
            blocks[c][r] = mixed[c * part : (c + 1) * part]
    source = partner(chip, step) * split + core
    filter_blocks([source * rows + r for r in range(rows)], blocks, mask_ref, table_ref, row_ref)


def arrived_blocks(raw, vertical_mix, polar_mask, tables, lon, rows, split, step):
    vmem = pl.BlockSpec(memory_space=pltpu.VMEM)
    return pl.pallas_call(
        functools.partial(arrived_kernel, rows, split, step),
        out_shape=[pltpu.VMEM((rows, vertical_mix.shape[1] // split, lon), F32)] * split,
        in_specs=[vmem, vmem, pl.BlockSpec(memory_space=pltpu.SMEM), vmem, vmem],
        out_specs=[vmem] * split,
        compiler_params=pltpu.CompilerParams(vmem_limit_bytes=VMEM_LIMIT),
        name="arrived_blocks",
    )(raw, vertical_mix, polar_mask, *tables)


def fill_slots(split, pick_ref, own_ref, first_ref, last_ref, out_ref):
    slots, flux_count, lon = out_ref.shape
    rows = own_ref.shape[0]
    upper = lax.rem(lax.axis_index("lat"), split) == 0
    for t in range(lon // LANES):
        lanes = slice(t * LANES, (t + 1) * LANES)
        first, last = ([ref[r, :, lanes] for r in range(rows)] for ref in (first_ref, last_ref))
        if split > 1:
            first, last = (
                [jnp.where(upper, outer, other) for outer, other in zip(last, first)],
                [jnp.where(upper, other, outer) for outer, other in zip(last, first)],
            )
        near = first + [own_ref[r, :, lanes] for r in range(rows)] + last
        for s in range(slots):
            pick = pick_ref[s]
            picked = jnp.zeros((flux_count, LANES), F32)
            for p, value in enumerate(near):
                picked = jnp.where(pick == p, value, picked)
            out_ref[s, :, lanes] = picked


def neighbour_rows(weighted, device_count):
    ends = device_count - 1
    return [
        lax.ppermute(weighted, "lat", [(i, i + 1) for i in range(ends)]),
        lax.ppermute(weighted, "lat", [(i + 1, i) for i in range(ends)]),
    ]


def ocean_slots(picks, weighted, near):
    vmem = pl.BlockSpec(memory_space=pltpu.VMEM)
    return pl.pallas_call(
        functools.partial(fill_slots, 1),
        out_shape=jax.ShapeDtypeStruct(picks.shape[:2] + weighted.shape[2:], F32),
        in_specs=[vmem] * 4,
        out_specs=vmem,
        compiler_params=pltpu.CompilerParams(vmem_limit_bytes=SMALL_LIMIT),
        name="ocean",
    )(picks, weighted, *near)


def place_kernel(split, sources, *refs):
    out_ref, ocean_ref, buffer, slots, sems, slots_sem = refs[-6:]
    surface = refs[-10:-6]
    part, lon = refs[0].shape[1:]
    rows = surface[1].shape[0]
    radix = lon // LANES
    chip_rows = rows * split
    tile = radix * SUBLANES
    me = lax.axis_index("lat")
    chip = me // split
    core = lax.rem(me, split)
    groups = chip_rows * len(sources) // SUBLANES
    chips = len(sources) // groups
    step_groups = [mask // chips for mask in STEPS] + [0]
    pending = [step_groups.count(group) for group in range(groups)]
    copies = []
    for step in [len(STEPS)] + list(range(len(STEPS))):
        source = partner(chip, step)
        base = source // chips * (part * tile) + lax.rem(source, chips) * chip_rows
        for c, operand in enumerate(sources[step]):
            ref = refs[operand]
            for r in range(ref.shape[0]):
                row = base + (r if len(sources[step]) == 1 else jnp.bitwise_xor(core, c) * rows + r)
                for t in range(radix):
                    buffer[pl.ds(row + t * SUBLANES, part, stride=tile), :] = ref[
                        r, :, t * LANES : (t + 1) * LANES
                    ]
        group = step_groups[step]
        pending[group] -= 1
        if not pending[group]:
            place = jnp.bitwise_xor(chip // chips, group)
            copy = pltpu.make_async_copy(
                buffer.at[pl.ds(pl.multiple_of(place * part * tile, SUBLANES), part * tile)].reshape(
                    part, tile, LANES
                ),
                out_ref.at[:, pl.ds(pl.multiple_of(place * tile, SUBLANES), tile)],
                sems.at[group],
            )
            copy.start()
            copies.append(copy)
    fill_slots(split, *surface, slots)
    copies.append(pltpu.make_async_copy(slots, ocean_ref, slots_sem))
    copies[-1].start()
    for copy in copies:
        copy.wait()


def place(operands, sources, lat_count, surface):
    part, lon = operands[0].shape[1:]
    size = part * lat_count * lon // LANES
    groups = lat_count // SUBLANES
    vmem = pl.BlockSpec(memory_space=pltpu.VMEM)
    slots = surface[0].shape[:2] + (lon,)
    out, ocean = pl.pallas_call(
        functools.partial(place_kernel, 2, sources),
        out_shape=[
            jax.ShapeDtypeStruct((part, size // part, LANES), F32),
            jax.ShapeDtypeStruct(slots, F32),
        ],
        in_specs=[vmem] * (len(operands) + len(surface)),
        out_specs=[pl.BlockSpec(memory_space=pltpu.HBM)] * 2,
        scratch_shapes=[
            pltpu.VMEM((size, LANES), F32),
            pltpu.VMEM(slots, F32),
            pltpu.SemaphoreType.DMA((groups,)),
            pltpu.SemaphoreType.DMA,
        ],
        compiler_params=pltpu.CompilerParams(vmem_limit_bytes=VMEM_LIMIT),
        name="place",
    )(*operands, *surface)
    tiles = out.reshape(part, groups, lon // LANES, SUBLANES, LANES)
    return tiles.transpose(0, 1, 3, 2, 4).reshape(part, lat_count, lon), ocean


def body(device_count, state, vertical_mix, coupling, fractions, weight_index, band_bounds, polar_mask):
    field_count, level_count = vertical_mix.shape[:2]
    stack_count, row_count, lon_count = state.shape
    lat_count = polar_mask.shape[0]
    part = stack_count // device_count
    tables = transform_tables(lon_count, lat_count)
    radix = lon_count // LANES
    blocked = with_layout_constraint(
        state.reshape(stack_count, row_count, radix, LANES), Layout(major_to_minor=(0, 2, 1, 3))
    )
    view = blocked.transpose(0, 2, 1, 3).reshape(-1, LANES)
    mixed = functools.partial(
        mixed_blocks,
        view,
        vertical_mix,
        polar_mask,
        band_bounds,
        coupling,
        fractions,
        weight_index,
        tables,
        lon_count,
        row_count,
    )

    if part == SUBLANES and level_count == 2 * part and field_count == len(STEPS) + 1:
        split = 2
        swap = [(i, i ^ 1) for i in range(device_count)]
        sibling = lax.ppermute(view, "lat", swap)
        raw = raw_fields(view, field_count, split, (0,))
        *blocks, weighted, picks = mixed((sibling,), 1)
        blocks = dict(enumerate(list(raw) + blocks))
        pairs = [(i, i + 1) for i in range(1, device_count - 1, 2)]
        pairs = {CORE: swap, OUTER: pairs + [(j, i) for i, j in pairs], FAR: swap}
        blocks |= {CORE: weighted, OUTER: weighted}
        for step in range(len(STEPS)):
            pairs[step] = [(i, split * partner(i // split, step) + i % split) for i in range(device_count)]
        for place_in_order, item in enumerate(ORDER):
            if item == FAR:
                blocks[0], blocks[FAR] = arrived_blocks(
                    blocks[0], vertical_mix, polar_mask, tables, lon_count, row_count, split, 0
                )
            if place_in_order >= WINDOW:
                earlier = ORDER[place_in_order - WINDOW]
                blocks[item], blocks[earlier] = lax.optimization_barrier((blocks[item], blocks[earlier]))
            blocks[item] = lax.ppermute(blocks[item], "lat", pairs[item])
        operands = [blocks[step] for step in range(len(STEPS) + 1)] + [blocks[FAR]]
        sources = [[0, len(STEPS) + 1]] + [[step] for step in range(1, len(STEPS) + 1)]
        surface = (picks, weighted, blocks[CORE], blocks[OUTER])
        state_out, ocean = place(operands, sources, lat_count, surface)
    else:
        *blocks, weighted, picks = mixed((), 0)
        stacked = jnp.concatenate(blocks, axis=1)
        moved = lax.all_to_all(stacked, "lat", split_axis=1, concat_axis=0, tiled=True)
        state_out = jnp.transpose(moved, (1, 0, 2))
        neighbours = neighbour_rows(weighted, device_count)
        ocean = ocean_slots(picks, weighted, neighbours)
    return (state_out, jnp.transpose(ocean, (1, 0, 2)))


def solution(mesh):
    return jax.shard_map(
        functools.partial(body, mesh.shape["lat"]),
        mesh=mesh,
        in_specs=(P("member", "lat", None), P(), P(), P(), P(("member", "lat")), P(), P()),
        out_specs=(P(("member", "lat"), None, None), P(None, ("member", "lat"), None)),
        check_vma=False,
    )
```
